128 devices in a mesh: tm: 16 (over z, x_lo, core), uly: 8 (over y, x_hi).
Axes of the slice: x: 4 (x_hi: 2, x_lo: 2; x = x_hi * 2 + x_lo), y: 4, z: 4, core: 2. Of those that a mesh axis runs over, the one named last changes fastest.
Arguments:
- queries: bfloat16 [12288, 5120], P(('tm', 'uly')), may hold values from -8 to 8
- keys: bfloat16 [12288, 5120], P(('tm', 'uly')), may hold values from -8 to 8
- values: bfloat16 [12288, 5120], P(('tm', 'uly')), may hold values from -6 to 6
- grad_out: bfloat16 [12288, 5120], P(('tm', 'uly')), may hold values from -6 to 6
Outputs:
- attended: bfloat16 [12288, 5120], P(('tm', 'uly'))
- grad_queries: bfloat16 [12288, 5120], P(('tm', 'uly'))
- grad_keys: bfloat16 [12288, 5120], P(('tm', 'uly'))
- grad_values: bfloat16 [12288, 5120], P(('tm', 'uly'))
The draws below stay inside these ranges and needn't reach their ends.
All inputs are finite; a program needn't handle non-finite values.
Results may differ from the reference program's by a relative error of at most 0.0096.
Values may be sent and summed in bfloat16 or wider, within the bound.
No kernel may reach another device: no remote copies, remote signals or barrier semaphores. Data moves between devices by JAX's collectives and lax.ppermute only.
A program may use at most 192 MiB of HBM per device.

```python
import jax
import jax.numpy as jnp
from jax import lax

HEADS = 40
HEAD_DIM = 128
D = 5120
GROUP = 768
WINDOW = 5
TOKENS = 12288


def draw_queries(key, part):
    key = jax.random.fold_in(key, 1)
    drawn = 1.5 * jnp.clip(jax.random.normal(key, (TOKENS, D)), -5.0, 5.0)
    return drawn.astype(jnp.bfloat16)


def draw_keys(key, part):
    key = jax.random.fold_in(key, 2)
    drawn = jnp.clip(jax.random.normal(key, (TOKENS, D)), -5.0, 5.0)
    return drawn.astype(jnp.bfloat16)


def levels(key, dims, shards, low, top_value):
    level, own = 1.0, jax.random.fold_in(key, 6)
    for position, parts in shards:
        heights = jnp.exp(jax.random.uniform(jax.random.fold_in(own, position), (parts,), jnp.float32, low / len(shards), top_value / len(shards)))
        level = level * jnp.repeat(heights, dims[position] // parts).reshape([-1 if axis == position else 1 for axis in range(len(dims))])
    return level


def scatter_about(key, extent, deviation, bound, pieces=(), kind=jnp.bfloat16):
    values = jax.random.normal(key, extent, jnp.float32) * deviation
    if len(pieces) > 0:
        values = levels(key, extent, pieces, -0.22, 0.18) * values
    return jnp.clip(values, min=-bound, max=bound).astype(kind)


def setup_inputs(seed: int = 0) -> dict:
    key_list = jax.random.split(jax.random.key(seed), 5)
    queries = draw_queries(jax.random.fold_in(key_list[4], 71), 0)
    keys = draw_keys(jax.random.fold_in(key_list[4], 71), 0)
    values = scatter_about(key_list[2], (TOKENS, D), 1.0, 6.0, ((0, 128),))
    grad_out = scatter_about(key_list[3], (TOKENS, D), 1.0, 6.0, ((0, 128),))
    return {"queries": queries, "keys": keys, "values": values, "grad_out": grad_out}


def attend(query_head, grad_head, key_head, value_head, allowed, kept_rows):
    factor = HEAD_DIM ** -0.5
    scores = jnp.dot(query_head, key_head.T, preferred_element_type=jnp.float32) * factor
    scores = jnp.where(allowed[None, :], scores, -jnp.inf)
    row_max = jnp.max(scores, axis=1, keepdims=True)
    row_sum = jnp.sum(jnp.exp(scores - row_max), axis=1, keepdims=True)
    log_norm = row_max + jnp.log(row_sum)
    weights = jnp.exp(scores - log_norm)
    weights_b = weights.astype(jnp.bfloat16)
    attended = jnp.dot(weights_b, value_head, preferred_element_type=jnp.float32)
    row_dot = jnp.sum(grad_head.astype(jnp.float32) * attended, axis=1)
    grad_weights = jnp.dot(grad_head, value_head.T, preferred_element_type=jnp.float32)
    grad_scores = (weights * (grad_weights - row_dot[:, None])).astype(jnp.bfloat16)
    grad_query = (jnp.dot(grad_scores, key_head, preferred_element_type=jnp.float32) * factor).astype(jnp.bfloat16)
    first = key_head.shape[0] - kept_rows
    grad_key = jnp.dot(grad_scores[:, first:].T, query_head, preferred_element_type=jnp.float32) * factor
    grad_value = jnp.dot(weights_b[:, first:].T, grad_head, preferred_element_type=jnp.float32)
    return attended.astype(jnp.bfloat16), grad_query, grad_key, grad_value, log_norm[:, 0], row_dot


def reference(queries, keys, values, grad_out):
    reach = WINDOW - 1
    group_count = TOKENS // GROUP

    def one_head(head_index):
        def column_slice(array):
            return lax.dynamic_slice_in_dim(array, head_index * HEAD_DIM, HEAD_DIM, 1)

        query_head = column_slice(queries)
        key_head = column_slice(keys)
        value_head = column_slice(values)
        grad_head = column_slice(grad_out)
        padding = jnp.zeros((reach * GROUP, HEAD_DIM), jnp.bfloat16)
        keys_padded = jnp.concatenate([padding, key_head], axis=0)
        values_padded = jnp.concatenate([padding, value_head], axis=0)
        zeros_acc = jnp.zeros(((group_count + reach) * GROUP, HEAD_DIM), jnp.float32)

        def advance(state_pair, group_id):
            key_acc, value_acc = state_pair
            start = (group_id * GROUP).astype(jnp.int32)
            query_block = lax.dynamic_slice_in_dim(query_head, start, GROUP, 0)
            grad_block = lax.dynamic_slice_in_dim(grad_head, start, GROUP, 0)
            key_block = lax.dynamic_slice_in_dim(keys_padded, start, WINDOW * GROUP, 0)
            value_block = lax.dynamic_slice_in_dim(values_padded, start, WINDOW * GROUP, 0)
            allowed = (jnp.arange(WINDOW * GROUP, dtype=jnp.int32) // GROUP + group_id - reach) >= 0
            attended, grad_query, grad_key, grad_value, log_norm, row_dot = attend(
                query_block, grad_block, key_block, value_block, allowed, WINDOW * GROUP)
            previous = lax.dynamic_slice_in_dim(key_acc, start, WINDOW * GROUP, 0)
            key_acc = lax.dynamic_update_slice_in_dim(key_acc, previous + grad_key, start, 0)
            previous = lax.dynamic_slice_in_dim(value_acc, start, WINDOW * GROUP, 0)
            value_acc = lax.dynamic_update_slice_in_dim(value_acc, previous + grad_value, start, 0)
            return (key_acc, value_acc), (attended, grad_query)

        (key_acc, value_acc), (attended_all, grad_query_all) = lax.scan(
            advance, (zeros_acc, zeros_acc), jnp.arange(group_count, dtype=jnp.int32))
        return (attended_all.reshape(TOKENS, HEAD_DIM), grad_query_all.reshape(TOKENS, HEAD_DIM),
                key_acc[reach * GROUP:].astype(jnp.bfloat16), value_acc[reach * GROUP:].astype(jnp.bfloat16))

    per_head = lax.map(one_head, jnp.arange(HEADS, dtype=jnp.int32))

    def merge_heads(array):
        return jnp.transpose(array, (1, 0, 2)).reshape(TOKENS, HEADS * HEAD_DIM)

    return (merge_heads(per_head[0]), merge_heads(per_head[1]), merge_heads(per_head[2]), merge_heads(per_head[3]))
```

```python
import functools
import math

import jax
import jax.numpy as jnp
from jax import lax
from jax.experimental import pallas as pl
from jax.experimental.pallas import tpu as pltpu
from jax.sharding import Mesh
from jax.sharding import PartitionSpec as P

HEAD_DIM = 128
WINDOW = 5
ROWS = 96
ULY = 8
QUAD = 4
GROUP = ROWS * ULY
TILE = 256
FACTOR = HEAD_DIM ** -0.5
LOG2E = math.log2(math.e)
PLANE = ("xl", "co", "y", "xh")
COLUMN = ("y", "xh")
TIME = ("z", "xl", "co")
ALL = ("z", "xl", "co", "y", "xh")
BF = jnp.bfloat16
F32 = jnp.float32


def dot(a, b, ca=1, cb=0):
    return lax.dot_general(a, b, (((ca,), (cb,)), ((), ())), preferred_element_type=F32)


def attention_tile(allowed, gi, row, q_s, g_s, k_s, v_s, kt_s, vt_s, dk_s, dv_s, s_s, p_s, o_s, dq_s):
    q = q_s[pl.ds(row, TILE), :]
    top = jnp.full((8, TILE), -jnp.inf, F32)
    for c in range(WINDOW):
        s = dot(k_s[gi + c], q, 1, 1)
        s_s[c] = s
        best = jnp.max(s.reshape(GROUP // 8, 8, TILE), axis=0)
        if c < WINDOW - 1:
            best = jnp.where(allowed(c), best, -jnp.inf)
        top = jnp.maximum(top, best)
    top = jnp.max(top, axis=0, keepdims=True)
    total = jnp.zeros((8, TILE), F32)
    out_t = jnp.zeros((HEAD_DIM, TILE), F32)
    for c in range(WINDOW):
        base = top if c == WINDOW - 1 else jnp.where(allowed(c), top, 1e30)
        p = jnp.exp2((s_s[c] - base) * (FACTOR * LOG2E))
        total = total + jnp.sum(p.reshape(GROUP // 8, 8, TILE), axis=0)
        pb = p.astype(BF)
        p_s[c] = pb
        out_t = out_t + dot(vt_s[gi + c], pb)
    inv = 1.0 / jnp.sum(total, axis=0, keepdims=True)
    out_t = out_t * inv
    g_t = g_s[pl.ds(row, TILE), :].astype(F32).T
    row_dot = jnp.sum(g_t * out_t, axis=0, keepdims=True) * inv
    g_t = g_t * inv
    g_tb = g_t.astype(BF)
    g_b = g_t.T.astype(BF)
    o_s[pl.ds(row, TILE), :] = out_t.T.astype(BF)
    dq_t = jnp.zeros((HEAD_DIM, TILE), F32)
    for c in range(WINDOW):
        dp = dot(v_s[gi + c], g_tb)
        pb = p_s[c]
        ds = (pb.astype(F32) * (dp - row_dot)).astype(BF)
        dq_t = dq_t + dot(kt_s[gi + c], ds)
        dk_s[gi + c] += dot(ds, q)
        dv_s[gi + c] += dot(pb, g_b)
    dq_s[pl.ds(row, TILE), :] = (dq_t * FACTOR).T.astype(BF)


def load_chunk(kv_ref, first, c, k_s, v_s, kt_s, vt_s):
    k = kv_ref[first:first + ULY, 0].reshape(GROUP, HEAD_DIM)
    v = kv_ref[first:first + ULY, 1].reshape(GROUP, HEAD_DIM)
    k_s[c] = k
    v_s[c] = v
    kt_s[c] = k.astype(F32).T.astype(BF)
    vt_s[c] = v.astype(F32).T.astype(BF)


def blocks(x):
    return x.reshape(x.shape[0] // ROWS, ROWS, HEAD_DIM)


def main_kernel(pos_ref, qg_ref, prev_ref, own_ref, od_ref, back_ref, mine_ref,
                q_s, g_s, k_s, v_s, kt_s, vt_s, dk_s, dv_s, s_s, p_s, o_s, dq_s):
    z = pos_ref[0]
    q_s[...] = qg_ref[:, 0].reshape(QUAD * GROUP, HEAD_DIM)
    g_s[...] = qg_ref[:, 1].reshape(QUAD * GROUP, HEAD_DIM)
    for c in range(QUAD):
        load_chunk(prev_ref, ULY * c, c, k_s, v_s, kt_s, vt_s)
        load_chunk(own_ref, ULY * c, QUAD + c, k_s, v_s, kt_s, vt_s)
    dk_s[...] = jnp.zeros_like(dk_s)
    dv_s[...] = jnp.zeros_like(dv_s)
    tiles = GROUP // TILE

    @pl.loop(0, QUAD * tiles)
    def _(i):
        gi = i // tiles
        attention_tile(lambda c: (z > 0) | (gi + c >= QUAD), gi, pl.multiple_of(i * TILE, TILE),
                       q_s, g_s, k_s, v_s, kt_s, vt_s, dk_s, dv_s, s_s, p_s, o_s, dq_s)

    od_ref[:, 0] = blocks(o_s[...])
    od_ref[:, 1] = blocks(dq_s[...])
    for c in range(QUAD):
        rows = slice(ULY * c, ULY * c + ULY)
        back_ref[rows, 0] = blocks((dk_s[c] * FACTOR).astype(BF))
        back_ref[rows, 1] = blocks(dv_s[c].astype(BF))
        mine_ref[rows, 0] = blocks(dk_s[QUAD + c] * FACTOR)
        mine_ref[rows, 1] = blocks(dv_s[QUAD + c])


def fifth_kernel(pos_ref, all_ref, e4_ref, e3_ref, e2_ref, e1_ref, od_ref, back_ref, mine_ref,
                 q_s, g_s, k_s, v_s, kt_s, vt_s, dk_s, dv_s, s_s, p_s, o_s, dq_s):
    t = pos_ref[0]
    q_s[...] = all_ref[:, 0].reshape(GROUP, HEAD_DIM)
    g_s[...] = all_ref[:, 1].reshape(GROUP, HEAD_DIM)
    for c, ref in enumerate((e4_ref, e3_ref, e2_ref, e1_ref)):
        load_chunk(ref, 0, c, k_s, v_s, kt_s, vt_s)
    load_chunk(all_ref.at[:, 2:4], 0, WINDOW - 1, k_s, v_s, kt_s, vt_s)
    dk_s[...] = jnp.zeros_like(dk_s)
    dv_s[...] = jnp.zeros_like(dv_s)

    @pl.loop(0, GROUP // TILE)
    def _(i):
        attention_tile(lambda c: t + c >= WINDOW - 1, 0, pl.multiple_of(i * TILE, TILE),
                       q_s, g_s, k_s, v_s, kt_s, vt_s, dk_s, dv_s, s_s, p_s, o_s, dq_s)

    od_ref[:, 0] = blocks(o_s[...])
    od_ref[:, 1] = blocks(dq_s[...])
    for c in range(WINDOW - 1):
        back_ref[c, :, 0] = blocks((dk_s[c] * FACTOR).astype(BF))
        back_ref[c, :, 1] = blocks(dv_s[c].astype(BF))
    mine_ref[:, 0] = blocks(dk_s[WINDOW - 1] * FACTOR)
    mine_ref[:, 1] = blocks(dv_s[WINDOW - 1])


def scratch(groups, chunks):
    rows = groups * GROUP
    return [
        pltpu.VMEM((rows, HEAD_DIM), BF),
        pltpu.VMEM((rows, HEAD_DIM), BF),
        pltpu.VMEM((chunks, GROUP, HEAD_DIM), BF),
        pltpu.VMEM((chunks, GROUP, HEAD_DIM), BF),
        pltpu.VMEM((chunks, HEAD_DIM, GROUP), BF),
        pltpu.VMEM((chunks, HEAD_DIM, GROUP), BF),
        pltpu.VMEM((chunks, GROUP, HEAD_DIM), F32),
        pltpu.VMEM((chunks, GROUP, HEAD_DIM), F32),
        pltpu.VMEM((WINDOW, GROUP, TILE), F32),
        pltpu.VMEM((WINDOW, GROUP, TILE), BF),
        pltpu.VMEM((rows, HEAD_DIM), BF),
        pltpu.VMEM((rows, HEAD_DIM), BF),
    ]


def cost(pairs):
    return pl.CostEstimate(flops=12 * pairs * GROUP * GROUP * HEAD_DIM,
                           bytes_accessed=pairs * 1000000, transcendentals=pairs * GROUP * GROUP)


SMEM = pl.BlockSpec(memory_space=pltpu.SMEM)
VMEM = pl.BlockSpec(memory_space=pltpu.VMEM)


def main_heads(pos, qg, prev, own):
    n = QUAD * ULY
    return pl.pallas_call(
        main_kernel,
        out_shape=(
            jax.ShapeDtypeStruct((n, 2, ROWS, HEAD_DIM), BF),
            jax.ShapeDtypeStruct((n, 2, ROWS, HEAD_DIM), BF),
            jax.ShapeDtypeStruct((n, 2, ROWS, HEAD_DIM), F32),
        ),
        in_specs=[SMEM, VMEM, VMEM, VMEM],
        out_specs=(VMEM, VMEM, VMEM),
        scratch_shapes=scratch(QUAD, 2 * QUAD),
        compiler_params=pltpu.CompilerParams(vmem_limit_bytes=56 * 2**20),
        cost_estimate=cost(20),
        name="main_heads",
    )(pos, qg, prev, own)


def fifth_head(pos, mine, e4, e3, e2, e1):
    return pl.pallas_call(
        fifth_kernel,
        out_shape=(
            jax.ShapeDtypeStruct((ULY, 2, ROWS, HEAD_DIM), BF),
            jax.ShapeDtypeStruct((WINDOW - 1, ULY, 2, ROWS, HEAD_DIM), BF),
            jax.ShapeDtypeStruct((ULY, 2, ROWS, HEAD_DIM), F32),
        ),
        in_specs=[SMEM] + [VMEM] * 5,
        out_specs=(VMEM, VMEM, VMEM),
        scratch_shapes=scratch(1, WINDOW),
        compiler_params=pltpu.CompilerParams(vmem_limit_bytes=56 * 2**20),
        cost_estimate=cost(5),
        name="fifth_head",
    )(pos, mine, e4, e3, e2, e1)


def exchange(x, axes):
    return lax.all_to_all(x, axes, 0, 0, tiled=True)


def shifted(x, axes, size, distance):
    return lax.ppermute(x, axes, [(i - distance, i) for i in range(size) if 0 <= i - distance < size])


def main_part(x):
    x = x.reshape(ROWS, ULY, WINDOW, HEAD_DIM)[:, :, :QUAD]
    return x.transpose(2, 1, 0, 3).reshape(QUAD * ULY, ROWS, HEAD_DIM)


def fifth_part(x):
    return x.reshape(ROWS, ULY, WINDOW, HEAD_DIM)[:, :, QUAD].transpose(1, 0, 2)


def join(main, fifth):
    main = main.reshape(QUAD, ULY, ROWS, HEAD_DIM)
    x = jnp.concatenate([main, fifth[None]], axis=0)
    return x.transpose(2, 1, 0, 3).reshape(ROWS, ULY * WINDOW * HEAD_DIM)


def per_device(queries, keys, values, grad_out):
    z = lax.axis_index("z")
    t = (z * 2 + lax.axis_index("xl")) * 2 + lax.axis_index("co")
    own = exchange(jnp.stack([main_part(keys), main_part(values)], axis=1), PLANE)
    prev = shifted(own, "z", 4, 1)
    qg = exchange(jnp.stack([main_part(queries), main_part(grad_out)], axis=1), PLANE)
    fifth = exchange(
        jnp.stack([fifth_part(a) for a in (queries, grad_out, keys, values)], axis=1), COLUMN)
    earlier = [shifted(fifth[:, 2:4], TIME, 16, d) for d in (4, 3, 2, 1)]

    od, back, mine = main_heads(z.reshape(1), qg, prev, own)
    od5, back5, mine5 = fifth_head(t.reshape(1), fifth, *earlier)

    dkv = (mine + shifted(back, "z", 4, -1)).astype(BF)
    dkv5 = mine5
    for c, d in enumerate((4, 3, 2, 1)):
        dkv5 = dkv5 + shifted(back5[c], TIME, 16, -d)
    od = exchange(od, PLANE)
    dkv = exchange(dkv, PLANE)
    fifth = exchange(jnp.concatenate([od5, dkv5.astype(BF)], axis=1), COLUMN)
    return (
        join(od[:, 0], fifth[:, 0]),
        join(od[:, 1], fifth[:, 1]),
        join(dkv[:, 0], fifth[:, 2]),
        join(dkv[:, 1], fifth[:, 3]),
    )


def solution(mesh):
    fine = Mesh(mesh.devices.reshape(4, 2, 2, 4, 2), ALL)
    spec = P(ALL, None)
    return jax.shard_map(per_device, mesh=fine, in_specs=(spec,) * 4, out_specs=(spec,) * 4, check_vma=False)
```

```python
import functools
import math

import jax
import jax.numpy as jnp
from jax import lax
from jax.experimental import pallas as pl
from jax.experimental.pallas import tpu as pltpu
from jax.sharding import Mesh
from jax.sharding import PartitionSpec as P

HEAD_DIM = 128
WINDOW = 5
ROWS = 96
ULY = 8
QUAD = 4
GROUP = ROWS * ULY
TILE = 768
FACTOR = HEAD_DIM ** -0.5
LOG2E = math.log2(math.e)
PLANE = ("xl", "co", "y", "xh")
COLUMN = ("y", "xh")
TIME = ("z", "xl", "co")
ALL = ("z", "xl", "co", "y", "xh")
BF = jnp.bfloat16
F32 = jnp.float32


def dot(a, b, ca=1, cb=0):
    return lax.dot_general(a, b, (((ca,), (cb,)), ((), ())), preferred_element_type=F32)


def attention_tile(allowed, gi, row, q_s, g_s, k_s, v_s, kt_s, vt_s, dk_s, dv_s, s_s, p_s, o_s, dq_s):
    q = q_s[pl.ds(row, TILE), :]
    top = jnp.full((8, TILE), -jnp.inf, F32)
    for c in range(WINDOW):
        s = dot(k_s[gi + c], q, 1, 1)
        s_s[c] = s
        best = jnp.max(s.reshape(GROUP // 8, 8, TILE), axis=0)
        if c < WINDOW - 1:
            best = jnp.where(allowed(c), best, -jnp.inf)
        top = jnp.maximum(top, best)
    top = jnp.max(top, axis=0, keepdims=True)
    total = jnp.zeros((8, TILE), F32)
    out_t = jnp.zeros((HEAD_DIM, TILE), F32)
    for c in range(WINDOW):
        base = top if c == WINDOW - 1 else jnp.where(allowed(c), top, 1e30)
        p = jnp.exp2((s_s[c] - base) * (FACTOR * LOG2E))
        total = total + jnp.sum(p.reshape(GROUP // 8, 8, TILE), axis=0)
        pb = p.astype(BF)
        p_s[c] = pb
        out_t = out_t + dot(vt_s[gi + c], pb)
    inv = 1.0 / jnp.sum(total, axis=0, keepdims=True)
    out_t = out_t * inv
    g_t = g_s[pl.ds(row, TILE), :].astype(F32).T
    row_dot = jnp.sum(g_t * out_t, axis=0, keepdims=True) * inv
    g_t = g_t * inv
    g_tb = g_t.astype(BF)
    q_t = q.astype(F32).T.astype(BF)
    o_s[pl.ds(row, TILE), :] = out_t.T.astype(BF)
    dq_t = jnp.zeros((HEAD_DIM, TILE), F32)
    for c in range(WINDOW):
        dp = dot(v_s[gi + c], g_tb)
        pb = p_s[c]
        ds = (pb.astype(F32) * (dp - row_dot)).astype(BF)
        dq_t = dq_t + dot(kt_s[gi + c], ds)
        dk_s[gi + c] += dot(q_t, ds, 1, 1)
        dv_s[gi + c] += dot(g_tb, pb, 1, 1)
    dq_s[pl.ds(row, TILE), :] = (dq_t * FACTOR).T.astype(BF)

def load_chunk(kv_ref, first, c, k_s, v_s, kt_s, vt_s):
    k = kv_ref[first:first + ULY, 0].reshape(GROUP, HEAD_DIM)
    v = kv_ref[first:first + ULY, 1].reshape(GROUP, HEAD_DIM)
    k_s[c] = k
    v_s[c] = v
    kt_s[c] = k.astype(F32).T.astype(BF)
    vt_s[c] = v.astype(F32).T.astype(BF)


def blocks(x):
    return x.reshape(x.shape[0] // ROWS, ROWS, HEAD_DIM)


def main_kernel(pos_ref, qg_ref, prev_ref, own_ref, od_ref, back_k_ref, back_v_ref, mine_ref,
                q_s, g_s, k_s, v_s, kt_s, vt_s, dk_s, dv_s, s_s, p_s, o_s, dq_s):
    z = pos_ref[0]
    q_s[...] = qg_ref[:, 0].reshape(QUAD * GROUP, HEAD_DIM)
    g_s[...] = qg_ref[:, 1].reshape(QUAD * GROUP, HEAD_DIM)
    for c in range(QUAD):
        load_chunk(prev_ref, ULY * c, c, k_s, v_s, kt_s, vt_s)
        load_chunk(own_ref, ULY * c, QUAD + c, k_s, v_s, kt_s, vt_s)
    dk_s[...] = jnp.zeros_like(dk_s)
    dv_s[...] = jnp.zeros_like(dv_s)
    tiles = GROUP // TILE

    @pl.loop(0, QUAD * tiles)
    def _(i):
        gi = i // tiles
        attention_tile(lambda c: (z > 0) | (gi + c >= QUAD), gi, pl.multiple_of(i * TILE, TILE),
                       q_s, g_s, k_s, v_s, kt_s, vt_s, dk_s, dv_s, s_s, p_s, o_s, dq_s)

    od_ref[:, 0] = blocks(o_s[...])
    od_ref[:, 1] = blocks(dq_s[...])
    for c in range(QUAD):
        rows = slice(ULY * c, ULY * c + ULY)
        back_k_ref[rows] = blocks((dk_s[c].T * FACTOR).astype(BF))
        back_v_ref[rows] = blocks(dv_s[c].T.astype(BF))
        mine_ref[rows, 0] = blocks(dk_s[QUAD + c].T * FACTOR)
        mine_ref[rows, 1] = blocks(dv_s[QUAD + c].T)


def fifth_kernel(flag_ref, all_ref, prev_ref, side_ref, core_ref, od_ref, mine_ref, b4_ref, b3_ref, b2_ref, b1_ref,
                 q_s, g_s, k_s, v_s, kt_s, vt_s, dk_s, dv_s, s_s, p_s, o_s, dq_s):
    q_s[...] = all_ref[:, 0].reshape(GROUP, HEAD_DIM)
    g_s[...] = all_ref[:, 1].reshape(GROUP, HEAD_DIM)
    for c, ref in enumerate((prev_ref, side_ref, core_ref.at[0], core_ref.at[1])):
        load_chunk(ref, 0, c, k_s, v_s, kt_s, vt_s)
    load_chunk(all_ref.at[:, 2:4], 0, WINDOW - 1, k_s, v_s, kt_s, vt_s)
    dk_s[...] = jnp.zeros_like(dk_s)
    dv_s[...] = jnp.zeros_like(dv_s)

    @pl.loop(0, GROUP // TILE)
    def _(i):
        attention_tile(lambda c: flag_ref[c] > 0, 0, pl.multiple_of(i * TILE, TILE),
                       q_s, g_s, k_s, v_s, kt_s, vt_s, dk_s, dv_s, s_s, p_s, o_s, dq_s)

    od_ref[:, 0] = blocks(o_s[...])
    od_ref[:, 1] = blocks(dq_s[...])
    mine_ref[:, 0] = blocks(dk_s[WINDOW - 1].T * FACTOR)
    mine_ref[:, 1] = blocks(dv_s[WINDOW - 1].T)
    far = jnp.where(flag_ref[4] == 0, 2, 3)
    for c, ref in ((0, b4_ref), (far, b3_ref), (1, b2_ref), (5 - far, b1_ref)):
        ref[:, 0] = blocks((dk_s[c].T * FACTOR).astype(BF))
        ref[:, 1] = blocks(dv_s[c].T.astype(BF))


def scratch(groups, chunks):
    rows = groups * GROUP
    return [
        pltpu.VMEM((rows, HEAD_DIM), BF),
        pltpu.VMEM((rows, HEAD_DIM), BF),
        pltpu.VMEM((chunks, GROUP, HEAD_DIM), BF),
        pltpu.VMEM((chunks, GROUP, HEAD_DIM), BF),
        pltpu.VMEM((chunks, HEAD_DIM, GROUP), BF),
        pltpu.VMEM((chunks, HEAD_DIM, GROUP), BF),
        pltpu.VMEM((chunks, HEAD_DIM, GROUP), F32),
        pltpu.VMEM((chunks, HEAD_DIM, GROUP), F32),
        pltpu.VMEM((WINDOW, GROUP, TILE), F32),
        pltpu.VMEM((WINDOW, GROUP, TILE), BF),
        pltpu.VMEM((rows, HEAD_DIM), BF),
        pltpu.VMEM((rows, HEAD_DIM), BF),
    ]


def cost(pairs):
    return pl.CostEstimate(flops=12 * pairs * GROUP * GROUP * HEAD_DIM,
                           bytes_accessed=pairs * 1000000, transcendentals=pairs * GROUP * GROUP)


SMEM = pl.BlockSpec(memory_space=pltpu.SMEM)
VMEM = pl.BlockSpec(memory_space=pltpu.VMEM)


def main_heads(pos, qg, prev, own):
    n = QUAD * ULY
    return pl.pallas_call(
        main_kernel,
        out_shape=(
            jax.ShapeDtypeStruct((n, 2, ROWS, HEAD_DIM), BF),
            jax.ShapeDtypeStruct((n, ROWS, HEAD_DIM), BF),
            jax.ShapeDtypeStruct((n, ROWS, HEAD_DIM), BF),
            jax.ShapeDtypeStruct((n, 2, ROWS, HEAD_DIM), F32),
        ),
        in_specs=[SMEM, VMEM, VMEM, VMEM],
        out_specs=(VMEM,) * 4,
        scratch_shapes=scratch(QUAD, 2 * QUAD),
        compiler_params=pltpu.CompilerParams(vmem_limit_bytes=56 * 2**20),
        cost_estimate=cost(20),
        name="main_heads",
    )(pos, qg, prev, own)


def fifth_head(flags, mine, prev, side, core):
    return pl.pallas_call(
        fifth_kernel,
        out_shape=(
            jax.ShapeDtypeStruct((ULY, 2, ROWS, HEAD_DIM), BF),
            jax.ShapeDtypeStruct((ULY, 2, ROWS, HEAD_DIM), F32),
        ) + (jax.ShapeDtypeStruct((ULY, 2, ROWS, HEAD_DIM), BF),) * 4,
        in_specs=[SMEM] + [VMEM] * 4,
        out_specs=(VMEM,) * 6,
        scratch_shapes=scratch(1, WINDOW),
        compiler_params=pltpu.CompilerParams(vmem_limit_bytes=56 * 2**20),
        cost_estimate=cost(5),
        name="fifth_head",
    )(flags, mine, prev, side, core)


def exchange(x, axes):
    return lax.all_to_all(x, axes, 0, 0, tiled=True)


def shifted(x, axes, size, distance):
    return lax.ppermute(x, axes, [(i - distance, i) for i in range(size) if 0 <= i - distance < size])


def pack_kernel(q_ref, g_ref, k_ref, v_ref, qg_ref, kv_ref, fifth_ref):
    for i, ref in enumerate((q_ref, g_ref, k_ref, v_ref)):
        main_ref = qg_ref if i < 2 else kv_ref
        for u in range(ULY):
            for j in range(WINDOW):
                col = (u * WINDOW + j) * HEAD_DIM
                piece = ref[:, col:col + HEAD_DIM]
                if j < QUAD:
                    main_ref[j * ULY + u, i % 2] = piece
                else:
                    fifth_ref[u, i] = piece


def packed(*arrays):
    main = jax.ShapeDtypeStruct((QUAD * ULY, 2, ROWS, HEAD_DIM), BF)
    fifth = jax.ShapeDtypeStruct((ULY, 4, ROWS, HEAD_DIM), BF)
    return pl.pallas_call(
        pack_kernel,
        out_shape=(main, main, fifth),
        in_specs=[VMEM] * 4,
        out_specs=(VMEM,) * 3,
        compiler_params=pltpu.CompilerParams(vmem_limit_bytes=56 * 2**20),
        cost_estimate=pl.CostEstimate(flops=0, bytes_accessed=2**23, transcendentals=0),
        name="pack",
    )(*arrays)


def combine_kernel(mine_ref, k_ref, v_ref, out_ref):
    out_ref[:, 0] = (mine_ref[:, 0] + k_ref[...].astype(F32)).astype(BF)
    out_ref[:, 1] = (mine_ref[:, 1] + v_ref[...].astype(F32)).astype(BF)


def combined(mine, k, v):
    n, step = QUAD * ULY, 8
    pair = pl.BlockSpec((step, 2, ROWS, HEAD_DIM), lambda i: (i, 0, 0, 0))
    one = pl.BlockSpec((step, ROWS, HEAD_DIM), lambda i: (i, 0, 0))
    return pl.pallas_call(
        combine_kernel,
        out_shape=jax.ShapeDtypeStruct((n, 2, ROWS, HEAD_DIM), BF),
        grid=(n // step,),
        in_specs=[pair, one, one],
        out_specs=pair,
        compiler_params=pltpu.CompilerParams(vmem_limit_bytes=24 * 2**20),
        cost_estimate=pl.CostEstimate(flops=0, bytes_accessed=2**23, transcendentals=0),
        name="combine",
    )(mine, k, v)


def unpack_kernel(first, main_ref, fifth_ref, *out_refs):
    for i, out_ref in enumerate(out_refs):
        for u in range(ULY):
            for j in range(WINDOW):
                col = (u * WINDOW + j) * HEAD_DIM
                out_ref[:, col:col + HEAD_DIM] = main_ref[j * ULY + u, i] if j < QUAD else fifth_ref[u, first + i]


def unpacked(main, fifth, first):
    out = jax.ShapeDtypeStruct((ROWS, ULY * WINDOW * HEAD_DIM), BF)
    return pl.pallas_call(
        functools.partial(unpack_kernel, first),
        out_shape=(out,) * 2,
        in_specs=[VMEM] * 2,
        out_specs=(VMEM,) * 2,
        compiler_params=pltpu.CompilerParams(vmem_limit_bytes=24 * 2**20),
        cost_estimate=pl.CostEstimate(flops=0, bytes_accessed=2**22, transcendentals=0),
        name="unpack",
    )(main, fifth)


def swapped(x, axis):
    return lax.ppermute(x, axis, [(0, 1), (1, 0)])


def per_device(queries, keys, values, grad_out):
    z, xl, co = lax.axis_index("z"), lax.axis_index("xl"), lax.axis_index("co")
    qg, kv, fifth = packed(queries, grad_out, keys, values)
    fifth = exchange(fifth, COLUMN)
    fifth, kv = lax.optimization_barrier((fifth, kv))
    own = exchange(kv, PLANE)
    own5 = fifth[:, 2:4]
    prev5 = shifted(own5, "z", 4, 1)
    side5 = swapped(jnp.where(xl == 0, own5, prev5), "xl")
    core5 = swapped(jnp.stack([jnp.where(co == 0, own5, prev5), side5]), "co")
    later = (z > 0).astype(jnp.int32)
    side_ok, core_ok = jnp.maximum(later, xl), jnp.maximum(later, co)
    flags = jnp.stack([later, side_ok, core_ok, side_ok, co])
    own, qg = lax.optimization_barrier((own, qg))
    prev = shifted(own, "z", 4, 1)
    qg = exchange(qg, PLANE)

    od5, mine5, *back5 = fifth_head(flags, fifth, prev5, side5, core5)
    own, od5, mine5, *back5 = lax.optimization_barrier((own, od5, mine5, *back5))
    back5 = [shifted(part, TIME, 16, -d) for d, part in zip((4, 3, 2, 1), back5)]

    od, back_k, back_v, mine = main_heads(z.reshape(1), qg, prev, own)
    od, back_k, back_v, *back5 = lax.optimization_barrier((od, back_k, back_v, *back5))
    got_k = shifted(back_k, "z", 4, -1)
    got_v = shifted(back_v, "z", 4, -1)
    od = exchange(od, PLANE)
    dkv5 = mine5
    for part in back5:
        dkv5 = dkv5 + part
    fifth = jnp.concatenate([od5, dkv5.astype(BF)], axis=1)
    od, got_k, fifth, mine = lax.optimization_barrier((od, got_k, fifth, mine))
    fifth = exchange(fifth, COLUMN)
    fifth, dkv = lax.optimization_barrier((fifth, combined(mine, got_k, got_v)))
    dkv = exchange(dkv, PLANE)
    return (*unpacked(od, fifth, 0), *unpacked(dkv, fifth, 2))


def solution(mesh):
    fine = Mesh(mesh.devices.reshape(4, 2, 2, 4, 2), ALL)
    spec = P(ALL, None)
    return jax.shard_map(per_device, mesh=fine, in_specs=(spec,) * 4, out_specs=(spec,) * 4, check_vma=False)
```

```python
import functools
import math

import jax
import jax.numpy as jnp
from jax import lax
from jax.experimental import pallas as pl
from jax.experimental.pallas import tpu as pltpu
from jax.sharding import Mesh
from jax.sharding import PartitionSpec as P

HEAD_DIM = 128
WINDOW = 5
ROWS = 96
ULY = 8
QUAD = 4
GROUP = ROWS * ULY
FACTOR = HEAD_DIM ** -0.5
LOG2E = math.log2(math.e)
PLANE = ("xl", "co", "y", "xh")
COLUMN = ("y", "xh")
TIME = ("z", "xl", "co")
ALL = ("z", "xl", "co", "y", "xh")
BF = jnp.bfloat16
F32 = jnp.float32


def dot(a, b, ca=1, cb=0):
    return lax.dot_general(a, b, (((ca,), (cb,)), ((), ())), preferred_element_type=F32)


def attend(allowed, gi, q, g, od_ref, k_s, v_s, kt_s, vt_s, dk_s, dv_s, s_s, p_s):
    top = jnp.full((8, GROUP), -jnp.inf, F32)
    for c in range(WINDOW):
        s = dot(k_s[gi + c], q, 1, 1)
        s_s[c] = s
        best = jnp.max(s.reshape(GROUP // 8, 8, GROUP), axis=0)
        if c < WINDOW - 1:
            best = jnp.where(allowed(c), best, -jnp.inf)
        top = jnp.maximum(top, best)
    top = jnp.max(top, axis=0, keepdims=True)
    total = jnp.zeros((8, GROUP), F32)
    out_t = jnp.zeros((HEAD_DIM, GROUP), F32)
    for c in range(WINDOW):
        base = top if c == WINDOW - 1 else jnp.where(allowed(c), top, 1e30)
        p = jnp.exp2((s_s[c] - base) * (FACTOR * LOG2E))
        total = total + jnp.sum(p.reshape(GROUP // 8, 8, GROUP), axis=0)
        pb = p.astype(BF)
        p_s[c] = pb
        out_t = out_t + dot(vt_s[gi + c], pb)
    inv = 1.0 / jnp.sum(total, axis=0, keepdims=True)
    out_t = out_t * inv
    g_t = g.astype(F32).T
    row_dot = jnp.sum(g_t * out_t, axis=0, keepdims=True) * inv
    g_tb = (g_t * inv).astype(BF)
    g_b = g_tb.T
    od_ref[:, 0] = blocks(out_t.T.astype(BF))
    dq_t = jnp.zeros((HEAD_DIM, GROUP), F32)
    for c in range(WINDOW):
        dp = dot(v_s[gi + c], g_tb)
        pb = p_s[c]
        ds = (pb.astype(F32) * (dp - row_dot)).astype(BF)
        dq_t = dq_t + dot(kt_s[gi + c], ds)
        dk_s[gi + c] += dot(ds, q)
        dv_s[gi + c] += dot(pb, g_b)
    od_ref[:, 1] = blocks((dq_t * FACTOR).T.astype(BF))


def load_chunk(kv_ref, c, k_s, v_s, kt_s, vt_s):
    k, v = flat(kv_ref[:, 0]), flat(kv_ref[:, 1])
    k_s[c] = k
    v_s[c] = v
    kt_s[c] = k.T
    vt_s[c] = v.T


def blocks(x):
    return x.reshape(ULY, ROWS, HEAD_DIM)


def flat(x):
    return x.reshape(GROUP, HEAD_DIM)


def main_kernel(pos_ref, qg_ref, prev_ref, own_ref, od_ref, back_k_ref, back_v_ref, mine_ref,
                k_s, v_s, kt_s, vt_s, dk_s, dv_s, s_s, p_s):
    gi = pl.program_id(0)
    z = pos_ref[0]

    @pl.when(gi == 0)
    def _():
        for c in range(QUAD):
            rows = slice(ULY * c, ULY * c + ULY)
            load_chunk(prev_ref.at[rows], c, k_s, v_s, kt_s, vt_s)
            load_chunk(own_ref.at[rows], QUAD + c, k_s, v_s, kt_s, vt_s)
        dk_s[...] = jnp.zeros_like(dk_s)
        dv_s[...] = jnp.zeros_like(dv_s)

    attend(lambda c: (z > 0) | (gi + c >= QUAD), gi, flat(qg_ref[:, 0]), flat(qg_ref[:, 1]), od_ref,
           k_s, v_s, kt_s, vt_s, dk_s, dv_s, s_s, p_s)
    back_k_ref[...] = blocks((dk_s[gi] * FACTOR).astype(BF))
    back_v_ref[...] = blocks(dv_s[gi].astype(BF))

    @pl.when(gi == QUAD - 1)
    def _():
        for c in range(QUAD):
            rows = slice(ULY * c, ULY * c + ULY)
            mine_ref[rows, 0] = blocks((dk_s[QUAD + c] * FACTOR).astype(BF))
            mine_ref[rows, 1] = blocks(dv_s[QUAD + c].astype(BF))


def fifth_kernel(flag_ref, all_ref, prev_ref, side_ref, core_ref, od_ref, mine_ref, b4_ref, b3_ref, b2_ref, b1_ref,
                 k_s, v_s, kt_s, vt_s, dk_s, dv_s, s_s, p_s):
    for c, ref in enumerate((prev_ref, side_ref, core_ref.at[0], core_ref.at[1], all_ref.at[:, 2:4])):
        load_chunk(ref, c, k_s, v_s, kt_s, vt_s)
    dk_s[...] = jnp.zeros_like(dk_s)
    dv_s[...] = jnp.zeros_like(dv_s)
    attend(lambda c: flag_ref[c] > 0, 0, flat(all_ref[:, 0]), flat(all_ref[:, 1]), od_ref,
           k_s, v_s, kt_s, vt_s, dk_s, dv_s, s_s, p_s)
    mine_ref[:, 0] = blocks(dk_s[WINDOW - 1] * FACTOR)
    mine_ref[:, 1] = blocks(dv_s[WINDOW - 1])
    far = jnp.where(flag_ref[4] == 0, 2, 3)
    for c, ref in ((0, b4_ref), (far, b3_ref), (1, b2_ref), (5 - far, b1_ref)):
        ref[:, 0] = blocks((dk_s[c] * FACTOR).astype(BF))
        ref[:, 1] = blocks(dv_s[c].astype(BF))


def scratch(chunks):
    return [
        pltpu.VMEM((chunks, GROUP, HEAD_DIM), BF),
        pltpu.VMEM((chunks, GROUP, HEAD_DIM), BF),
        pltpu.VMEM((chunks, HEAD_DIM, GROUP), BF),
        pltpu.VMEM((chunks, HEAD_DIM, GROUP), BF),
        pltpu.VMEM((chunks, GROUP, HEAD_DIM), F32),
        pltpu.VMEM((chunks, GROUP, HEAD_DIM), F32),
        pltpu.VMEM((WINDOW, GROUP, GROUP), F32),
        pltpu.VMEM((WINDOW, GROUP, GROUP), BF),
    ]


def cost(pairs):
    return pl.CostEstimate(flops=12 * pairs * GROUP * GROUP * HEAD_DIM,
                           bytes_accessed=pairs * 1000000, transcendentals=pairs * GROUP * GROUP)


def params(grid=False):
    return pltpu.CompilerParams(
        vmem_limit_bytes=56 * 2**20, dimension_semantics=("arbitrary",) if grid else None)


def bf(*dims):
    return jax.ShapeDtypeStruct((*dims, ROWS, HEAD_DIM), BF)


SMEM = pl.BlockSpec(memory_space=pltpu.SMEM)
VMEM = pl.BlockSpec(memory_space=pltpu.VMEM)


def main_heads(pos, qg, prev, own):
    n = QUAD * ULY
    group = pl.BlockSpec((ULY, 2, ROWS, HEAD_DIM), lambda i: (i, 0, 0, 0))
    one = pl.BlockSpec((ULY, ROWS, HEAD_DIM), lambda i: (i, 0, 0))
    whole = pl.BlockSpec((n, 2, ROWS, HEAD_DIM), lambda i: (0, 0, 0, 0))
    return pl.pallas_call(
        main_kernel,
        out_shape=(bf(n, 2), bf(n), bf(n), bf(n, 2)),
        grid=(QUAD,),
        in_specs=[SMEM, group, whole, whole],
        out_specs=(group, one, one, whole),
        scratch_shapes=scratch(2 * QUAD),
        compiler_params=params(True),
        cost_estimate=cost(20),
        name="main_heads",
    )(pos, qg, prev, own)


def fifth_head(flags, mine, prev, side, core):
    return pl.pallas_call(
        fifth_kernel,
        out_shape=(bf(ULY, 2), jax.ShapeDtypeStruct((ULY, 2, ROWS, HEAD_DIM), F32)) + (bf(ULY, 2),) * 4,
        in_specs=[SMEM] + [VMEM] * 4,
        out_specs=(VMEM,) * 6,
        scratch_shapes=scratch(WINDOW),
        compiler_params=params(),
        cost_estimate=cost(5),
        name="fifth_head",
    )(flags, mine, prev, side, core)


def exchange(x, axes):
    return lax.all_to_all(x, axes, 0, 0, tiled=True)


def shifted(x, axes, size, distance):
    return lax.ppermute(x, axes, [(i - distance, i) for i in range(size) if 0 <= i - distance < size])


def pack_kernel(q_ref, g_ref, k_ref, v_ref, qg_ref, kv_ref, fifth_ref):
    for i, ref in enumerate((q_ref, g_ref, k_ref, v_ref)):
        main_ref = qg_ref if i < 2 else kv_ref
        for u in range(ULY):
            for j in range(WINDOW):
                col = (u * WINDOW + j) * HEAD_DIM
                piece = ref[:, col:col + HEAD_DIM]
                if j < QUAD:
                    main_ref[j * ULY + u, i % 2] = piece
                else:
                    fifth_ref[u, i] = piece


def unpack_kernel(first, main_ref, fifth_ref, *out_refs):
    for i, out_ref in enumerate(out_refs):
        for u in range(ULY):
            for j in range(WINDOW):
                col = (u * WINDOW + j) * HEAD_DIM
                out_ref[:, col:col + HEAD_DIM] = main_ref[j * ULY + u, i] if j < QUAD else fifth_ref[u, first + i]


def combine_kernel(mine_ref, k_ref, v_ref, out_ref):
    out_ref[:, 0] = (mine_ref[:, 0].astype(F32) + k_ref[...].astype(F32)).astype(BF)
    out_ref[:, 1] = (mine_ref[:, 1].astype(F32) + v_ref[...].astype(F32)).astype(BF)


def finish_kernel(od_ref, mine_ref, b4_ref, b3_ref, b2_ref, b1_ref, out_ref):
    out_ref[:, 0:2] = od_ref[...]
    total = mine_ref[...]
    for ref in (b4_ref, b3_ref, b2_ref, b1_ref):
        total = total + ref[...].astype(F32)
    out_ref[:, 2:4] = total.astype(BF)


def moved(kernel, name, out_shape, *arrays, limit=24):
    return pl.pallas_call(
        kernel,
        out_shape=tuple(out_shape),
        in_specs=[VMEM] * len(arrays),
        out_specs=(VMEM,) * len(out_shape),
        compiler_params=pltpu.CompilerParams(vmem_limit_bytes=limit * 2**20),
        cost_estimate=pl.CostEstimate(flops=0, bytes_accessed=2**22, transcendentals=0),
        name=name,
    )(*arrays)


def packed(*arrays):
    n = QUAD * ULY
    return moved(pack_kernel, "pack", [bf(n, 2)] * 2 + [bf(ULY, 4)], *arrays, limit=56)


def unpacked(main, fifth, first):
    out = jax.ShapeDtypeStruct((ROWS, ULY * WINDOW * HEAD_DIM), BF)
    return moved(functools.partial(unpack_kernel, first), "unpack", [out] * 2, main, fifth)


def combined(*arrays):
    return moved(combine_kernel, "combine", [bf(QUAD * ULY, 2)], *arrays)[0]


def swapped(x, axis):
    return lax.ppermute(x, axis, [(0, 1), (1, 0)])


def per_device(queries, keys, values, grad_out):
    z, xl, co = lax.axis_index("z"), lax.axis_index("xl"), lax.axis_index("co")
    qg, kv, fifth = packed(queries, grad_out, keys, values)
    fifth = exchange(fifth, COLUMN)
    fifth, kv = lax.optimization_barrier((fifth, kv))
    own = exchange(kv, PLANE)
    own5 = fifth[:, 2:4]
    prev5 = shifted(own5, "z", 4, 1)
    side5 = swapped(jnp.where(xl == 0, own5, prev5), "xl")
    core5 = swapped(jnp.stack([jnp.where(co == 0, own5, prev5), side5]), "co")
    later = (z > 0).astype(jnp.int32)
    side_ok, core_ok = jnp.maximum(later, xl), jnp.maximum(later, co)
    flags = jnp.stack([later, side_ok, core_ok, side_ok, co])
    own, qg = lax.optimization_barrier((own, qg))
    prev = shifted(own, "z", 4, 1)
    qg = exchange(qg, PLANE)

    od5, mine5, *back5 = fifth_head(flags, fifth, prev5, side5, core5)
    own, od5, mine5, *back5 = lax.optimization_barrier((own, od5, mine5, *back5))
    back5 = [shifted(part, TIME, 16, -d) for d, part in zip((4, 3, 2, 1), back5)]

    od, back_k, back_v, mine = main_heads(z.reshape(1), qg, prev, own)
    od, back_k, back_v, *back5 = lax.optimization_barrier((od, back_k, back_v, *back5))
    got_k = shifted(back_k, "z", 4, -1)
    got_v = shifted(back_v, "z", 4, -1)
    fifth = moved(finish_kernel, "finish", [bf(ULY, 4)], od5, mine5, *back5)[0]
    od, fifth = lax.optimization_barrier((od, fifth))
    od = exchange(od, PLANE)
    od, got_k, fifth, mine = lax.optimization_barrier((od, got_k, fifth, mine))
    fifth = exchange(fifth, COLUMN)
    fifth, dkv = lax.optimization_barrier((fifth, combined(mine, got_k, got_v)))
    dkv = exchange(dkv, PLANE)
    return (*unpacked(od, fifth, 0), *unpacked(dkv, fifth, 2))


def solution(mesh):
    fine = Mesh(mesh.devices.reshape(4, 2, 2, 4, 2), ALL)
    spec = P(ALL, None)
    return jax.shard_map(per_device, mesh=fine, in_specs=(spec,) * 4, out_specs=(spec,) * 4, check_vma=False)
```

```python
import functools
import math

import jax
import jax.numpy as jnp
from jax import lax
from jax.experimental import pallas as pl
from jax.experimental.pallas import tpu as pltpu
from jax.sharding import Mesh
from jax.sharding import PartitionSpec as P

HEAD_DIM = 128
WINDOW = 5
ROWS = 96
ULY = 8
QUAD = 4
GROUP = ROWS * ULY
FACTOR = HEAD_DIM ** -0.5
LOG2E = math.log2(math.e)
PLANE = ("xl", "co", "y", "xh")
COLUMN = ("y", "xh")
TIME = ("z", "xl", "co")
ALL = ("z", "xl", "co", "y", "xh")
BF = jnp.bfloat16
F32 = jnp.float32


def dot(a, b, ca=1, cb=0):
    return lax.dot_general(a, b, (((ca,), (cb,)), ((), ())), preferred_element_type=F32)


def attend(allowed, gi, q, g, od_ref, k_s, v_s, kt_s, vt_s, dk_s, dv_s, s_s, p_s):
    top = jnp.full((8, GROUP), -jnp.inf, F32)
    for c in range(WINDOW):
        s = dot(k_s[gi + c], q, 1, 1)
        s_s[c] = s
        best = jnp.max(s.reshape(GROUP // 8, 8, GROUP), axis=0)
        if c < WINDOW - 1:
            best = jnp.where(allowed(c), best, -jnp.inf)
        top = jnp.maximum(top, best)
    top = jnp.max(top, axis=0, keepdims=True)
    total = jnp.zeros((8, GROUP), F32)
    out_t = jnp.zeros((HEAD_DIM, GROUP), F32)
    for c in range(WINDOW):
        base = top if c == WINDOW - 1 else jnp.where(allowed(c), top, 1e30)
        p = jnp.exp2((s_s[c] - base) * (FACTOR * LOG2E))
        total = total + jnp.sum(p.reshape(GROUP // 8, 8, GROUP), axis=0)
        pb = p.astype(BF)
        p_s[c] = pb
        out_t = out_t + dot(vt_s[gi + c], pb)
    inv = 1.0 / jnp.sum(total, axis=0, keepdims=True)
    out_t = out_t * inv
    g_t = g.astype(F32).T
    row_dot = jnp.sum(g_t * out_t, axis=0, keepdims=True) * inv
    g_tb = (g_t * inv).astype(BF)
    g_b = g_tb.T
    od_ref[:, 0] = blocks(out_t.T.astype(BF))
    dq_t = jnp.zeros((HEAD_DIM, GROUP), F32)
    for c in range(WINDOW):
        dp = dot(v_s[gi + c], g_tb)
        pb = p_s[c]
        ds = (pb.astype(F32) * (dp - row_dot)).astype(BF)
        dq_t = dq_t + dot(kt_s[gi + c], ds)
        if c < WINDOW - 1:
            dk_s[gi + c] += dot(ds, q)
            dv_s[gi + c] += dot(pb, g_b)
        else:
            dk_s[gi + c] = dot(ds, q)
            dv_s[gi + c] = dot(pb, g_b)
    od_ref[:, 1] = blocks((dq_t * FACTOR).T.astype(BF))


def load_chunk(kv_ref, c, k_s, v_s, kt_s, vt_s):
    k, v = flat(kv_ref[:, 0]), flat(kv_ref[:, 1])
    k_s[c] = k
    v_s[c] = v
    kt_s[c] = k.T
    vt_s[c] = v.T


def blocks(x):
    return x.reshape(ULY, ROWS, HEAD_DIM)


def flat(x):
    return x.reshape(GROUP, HEAD_DIM)


def main_kernel(pos_ref, qg_ref, prev_ref, own_ref, od_ref, back_k_ref, back_v_ref, mine_ref,
                k_s, v_s, kt_s, vt_s, dk_s, dv_s, s_s, p_s):
    gi = pl.program_id(0)
    z = pos_ref[0]

    @pl.when(gi == 0)
    def _():
        for c in range(QUAD):
            rows = slice(ULY * c, ULY * c + ULY)
            load_chunk(prev_ref.at[rows], c, k_s, v_s, kt_s, vt_s)
            load_chunk(own_ref.at[rows], QUAD + c, k_s, v_s, kt_s, vt_s)
        dk_s[:QUAD] = jnp.zeros((QUAD, GROUP, HEAD_DIM), F32)
        dv_s[:QUAD] = jnp.zeros((QUAD, GROUP, HEAD_DIM), F32)

    attend(lambda c: (z > 0) | (gi + c >= QUAD), gi, flat(qg_ref[:, 0]), flat(qg_ref[:, 1]), od_ref,
           k_s, v_s, kt_s, vt_s, dk_s, dv_s, s_s, p_s)
    back_k_ref[...] = blocks((dk_s[gi] * FACTOR).astype(BF))
    back_v_ref[...] = blocks(dv_s[gi].astype(BF))

    @pl.when(gi == QUAD - 1)
    def _():
        for c in range(QUAD):
            rows = slice(ULY * c, ULY * c + ULY)
            mine_ref[rows, 0] = blocks((dk_s[QUAD + c] * FACTOR).astype(BF))
            mine_ref[rows, 1] = blocks(dv_s[QUAD + c].astype(BF))


def fifth_kernel(flag_ref, all_ref, prev_ref, side_ref, core_ref, od_ref, mine_ref, b4_ref, b3_ref, b2_ref, b1_ref,
                 k_s, v_s, kt_s, vt_s, dk_s, dv_s, s_s, p_s):
    for c, ref in enumerate((prev_ref, side_ref, core_ref.at[0], core_ref.at[1], all_ref.at[:, 2:4])):
        load_chunk(ref, c, k_s, v_s, kt_s, vt_s)
    dk_s[:QUAD] = jnp.zeros((QUAD, GROUP, HEAD_DIM), F32)
    dv_s[:QUAD] = jnp.zeros((QUAD, GROUP, HEAD_DIM), F32)
    attend(lambda c: flag_ref[c] > 0, 0, flat(all_ref[:, 0]), flat(all_ref[:, 1]), od_ref,
           k_s, v_s, kt_s, vt_s, dk_s, dv_s, s_s, p_s)
    mine_ref[:, 0] = blocks(dk_s[WINDOW - 1] * FACTOR)
    mine_ref[:, 1] = blocks(dv_s[WINDOW - 1])
    far = jnp.where(flag_ref[4] == 0, 2, 3)
    for c, ref in ((0, b4_ref), (far, b3_ref), (1, b2_ref), (5 - far, b1_ref)):
        ref[:, 0] = blocks((dk_s[c] * FACTOR).astype(BF))
        ref[:, 1] = blocks(dv_s[c].astype(BF))


def scratch(chunks):
    return [
        pltpu.VMEM((chunks, GROUP, HEAD_DIM), BF),
        pltpu.VMEM((chunks, GROUP, HEAD_DIM), BF),
        pltpu.VMEM((chunks, HEAD_DIM, GROUP), BF),
        pltpu.VMEM((chunks, HEAD_DIM, GROUP), BF),
        pltpu.VMEM((chunks, GROUP, HEAD_DIM), F32),
        pltpu.VMEM((chunks, GROUP, HEAD_DIM), F32),
        pltpu.VMEM((WINDOW, GROUP, GROUP), F32),
        pltpu.VMEM((WINDOW, GROUP, GROUP), BF),
    ]


def cost(pairs):
    return pl.CostEstimate(flops=12 * pairs * GROUP * GROUP * HEAD_DIM,
                           bytes_accessed=pairs * 1000000, transcendentals=pairs * GROUP * GROUP)


def params(grid=False):
    return pltpu.CompilerParams(
        vmem_limit_bytes=56 * 2**20, dimension_semantics=("arbitrary",) if grid else None)


def bf(*dims):
    return jax.ShapeDtypeStruct((*dims, ROWS, HEAD_DIM), BF)


SMEM = pl.BlockSpec(memory_space=pltpu.SMEM)
VMEM = pl.BlockSpec(memory_space=pltpu.VMEM)


def main_heads(pos, qg, prev, own):
    n = QUAD * ULY
    group = pl.BlockSpec((ULY, 2, ROWS, HEAD_DIM), lambda i: (i, 0, 0, 0))
    one = pl.BlockSpec((ULY, ROWS, HEAD_DIM), lambda i: (i, 0, 0))
    whole = pl.BlockSpec((n, 2, ROWS, HEAD_DIM), lambda i: (0, 0, 0, 0))
    return pl.pallas_call(
        main_kernel,
        out_shape=(bf(n, 2), bf(n), bf(n), bf(n, 2)),
        grid=(QUAD,),
        in_specs=[SMEM, group, whole, whole],
        out_specs=(group, one, one, whole),
        scratch_shapes=scratch(2 * QUAD),
        compiler_params=params(True),
        cost_estimate=cost(20),
        name="main_heads",
    )(pos, qg, prev, own)


def fifth_head(flags, mine, prev, side, core):
    return pl.pallas_call(
        fifth_kernel,
        out_shape=(bf(ULY, 2), jax.ShapeDtypeStruct((ULY, 2, ROWS, HEAD_DIM), F32)) + (bf(ULY, 2),) * 4,
        in_specs=[SMEM] + [VMEM] * 4,
        out_specs=(VMEM,) * 6,
        scratch_shapes=scratch(WINDOW),
        compiler_params=params(),
        cost_estimate=cost(5),
        name="fifth_head",
    )(flags, mine, prev, side, core)


def exchange(x, axes):
    return lax.all_to_all(x, axes, 0, 0, tiled=True)


def shifted(x, axes, size, distance):
    return lax.ppermute(x, axes, [(i - distance, i) for i in range(size) if 0 <= i - distance < size])


def pack_kernel(q_ref, g_ref, k_ref, v_ref, qg_ref, kv_ref):
    for i, ref in enumerate((q_ref, g_ref, k_ref, v_ref)):
        main_ref = qg_ref if i < 2 else kv_ref
        for u in range(ULY):
            for j in range(QUAD):
                col = (u * WINDOW + j) * HEAD_DIM
                main_ref[j * ULY + u, i % 2] = ref[:, col:col + HEAD_DIM]


def pack_fifth_kernel(q_ref, g_ref, k_ref, v_ref, fifth_ref):
    for i, ref in enumerate((q_ref, g_ref, k_ref, v_ref)):
        for u in range(ULY):
            col = (u * WINDOW + QUAD) * HEAD_DIM
            fifth_ref[u, i] = ref[:, col:col + HEAD_DIM]


def unpack_kernel(first, main_ref, fifth_ref, *out_refs):
    for i, out_ref in enumerate(out_refs):
        for u in range(ULY):
            for j in range(WINDOW):
                col = (u * WINDOW + j) * HEAD_DIM
                out_ref[:, col:col + HEAD_DIM] = main_ref[j * ULY + u, i] if j < QUAD else fifth_ref[u, first + i]


def combine_kernel(mine_ref, k_ref, v_ref, out_ref):
    out_ref[:, 0] = (mine_ref[:, 0].astype(F32) + k_ref[...].astype(F32)).astype(BF)
    out_ref[:, 1] = (mine_ref[:, 1].astype(F32) + v_ref[...].astype(F32)).astype(BF)


def finish_kernel(od_ref, mine_ref, b4_ref, b3_ref, b2_ref, b1_ref, out_ref):
    out_ref[:, 0:2] = od_ref[...]
    total = mine_ref[...]
    for ref in (b4_ref, b3_ref, b2_ref, b1_ref):
        total = total + ref[...].astype(F32)
    out_ref[:, 2:4] = total.astype(BF)


def moved(kernel, name, out_shape, *arrays, limit=24):
    return pl.pallas_call(
        kernel,
        out_shape=tuple(out_shape),
        in_specs=[VMEM] * len(arrays),
        out_specs=(VMEM,) * len(out_shape),
        compiler_params=pltpu.CompilerParams(vmem_limit_bytes=limit * 2**20),
        cost_estimate=pl.CostEstimate(flops=0, bytes_accessed=2**22, transcendentals=0),
        name=name,
    )(*arrays)


def packed(*arrays):
    n = QUAD * ULY
    return moved(pack_kernel, "pack", [bf(n, 2)] * 2, *arrays, limit=56)


def packed_fifth(*arrays):
    return moved(pack_fifth_kernel, "pack_fifth", [bf(ULY, 4)], *arrays, limit=56)[0]


def unpacked(main, fifth, first):
    out = jax.ShapeDtypeStruct((ROWS, ULY * WINDOW * HEAD_DIM), BF)
    return moved(functools.partial(unpack_kernel, first), "unpack", [out] * 2, main, fifth)


def combined(*arrays):
    return moved(combine_kernel, "combine", [bf(QUAD * ULY, 2)], *arrays, limit=56)[0]


def swapped(x, axis):
    return lax.ppermute(x, axis, [(0, 1), (1, 0)])


def per_device(queries, keys, values, grad_out):
    z, xl, co = lax.axis_index("z"), lax.axis_index("xl"), lax.axis_index("co")
    fifth = exchange(packed_fifth(queries, grad_out, keys, values), COLUMN)
    qg, kv = packed(queries, grad_out, keys, values)
    fifth, kv = lax.optimization_barrier((fifth, kv))
    own = exchange(kv, PLANE)
    own5 = fifth[:, 2:4]
    prev5 = shifted(own5, "z", 4, 1)
    side5 = swapped(jnp.where(xl == 0, own5, prev5), "xl")
    core5 = swapped(jnp.stack([jnp.where(co == 0, own5, prev5), side5]), "co")
    later = (z > 0).astype(jnp.int32)
    side_ok, core_ok = jnp.maximum(later, xl), jnp.maximum(later, co)
    flags = jnp.stack([later, side_ok, core_ok, side_ok, co])
    own, qg = lax.optimization_barrier((own, qg))
    prev = shifted(own, "z", 4, 1)
    qg = exchange(qg, PLANE)

    od5, mine5, *back5 = fifth_head(flags, fifth, prev5, side5, core5)
    own, od5, mine5, *back5 = lax.optimization_barrier((own, od5, mine5, *back5))
    back5 = [shifted(part, TIME, 16, -d) for d, part in zip((4, 3, 2, 1), back5)]

    od, back_k, back_v, mine = main_heads(z.reshape(1), qg, prev, own)
    od, back_k, back_v, *back5 = lax.optimization_barrier((od, back_k, back_v, *back5))
    got_k = shifted(back_k, "z", 4, -1)
    got_v = shifted(back_v, "z", 4, -1)
    fifth = moved(finish_kernel, "finish", [bf(ULY, 4)], od5, mine5, *back5)[0]
    od, fifth = lax.optimization_barrier((od, fifth))
    od = exchange(od, PLANE)
    od, got_k, fifth, mine = lax.optimization_barrier((od, got_k, fifth, mine))
    fifth = exchange(fifth, COLUMN)
    fifth, dkv = lax.optimization_barrier((fifth, combined(mine, got_k, got_v)))
    dkv = exchange(dkv, PLANE)
    return (*unpacked(od, fifth, 0), *unpacked(dkv, fifth, 2))


def solution(mesh):
    fine = Mesh(mesh.devices.reshape(4, 2, 2, 4, 2), ALL)
    spec = P(ALL, None)
    return jax.shard_map(per_device, mesh=fine, in_specs=(spec,) * 4, out_specs=(spec,) * 4, check_vma=False)
```

```python
import functools
import math

import jax
import jax.numpy as jnp
from jax import lax
from jax.experimental import pallas as pl
from jax.experimental.pallas import tpu as pltpu
from jax.sharding import Mesh
from jax.sharding import PartitionSpec as P

HEAD_DIM = 128
WINDOW = 5
ROWS = 96
ULY = 8
QUAD = 4
GROUP = ROWS * ULY
WIDE = HEAD_DIM + 16
FACTOR = HEAD_DIM ** -0.5
LOG2E = math.log2(math.e)
PLANE = ("xl", "co", "y", "xh")
COLUMN = ("y", "xh")
TIME = ("z", "xl", "co")
ALL = ("z", "xl", "co", "y", "xh")
BF = jnp.bfloat16
F32 = jnp.float32


def dot(a, b, ca=1, cb=0):
    return lax.dot_general(a, b, (((ca,), (cb,)), ((), ())), preferred_element_type=F32)


def attend(allowed, gi, q, g, od_ref, k_s, v_s, kt_s, vt_s, dk_s, dv_s, s_s, p_s):
    top = jnp.full((8, GROUP), -jnp.inf, F32)
    for c in range(WINDOW):
        s = dot(k_s[gi + c], q, 1, 1)
        s_s[c] = s
        best = jnp.max(s.reshape(GROUP // 8, 8, GROUP), axis=0)
        if c < WINDOW - 1:
            best = jnp.where(allowed(c), best, -jnp.inf)
        top = jnp.maximum(top, best)
    top = jnp.max(top, axis=0, keepdims=True)
    out_t = jnp.zeros((WIDE, GROUP), F32)
    for c in range(WINDOW):
        base = top if c == WINDOW - 1 else jnp.where(allowed(c), top, 1e30)
        p = jnp.exp2((s_s[c] - base) * (FACTOR * LOG2E))
        pb = p.astype(BF)
        p_s[c] = pb
        out_t = out_t + dot(vt_s[gi + c], pb)
    inv = 1.0 / out_t[HEAD_DIM:HEAD_DIM + 1]
    out_t = out_t[:HEAD_DIM] * inv
    g_t = g.astype(F32).T
    row_dot = jnp.sum(g_t * out_t, axis=0, keepdims=True) * inv
    g_tb = (g_t * inv).astype(BF)
    g_b = g_tb.T
    od_ref[:, 0] = blocks(out_t.T.astype(BF))
    dq_t = jnp.zeros((HEAD_DIM, GROUP), F32)
    dp = dot(v_s[gi], g_tb)
    for c in range(WINDOW):
        pb = p_s[c]
        ds = (pb.astype(F32) * (dp - row_dot)).astype(BF)
        if c < WINDOW - 1:
            dp = dot(v_s[gi + c + 1], g_tb)
            dv_s[gi + c] += dot(pb, g_b)
            dk_s[gi + c] += dot(ds, q)
        else:
            dv_s[gi + c] = dot(pb, g_b)
            dk_s[gi + c] = dot(ds, q)
        dq_t = dq_t + dot(kt_s[gi + c], ds)
    od_ref[:, 1] = blocks((dq_t * FACTOR).T.astype(BF))


def load_chunk(kv_ref, c, k_s, v_s, kt_s, vt_s):
    k, v = flat(kv_ref[:, 0]), flat(kv_ref[:, 1])
    k_s[c] = k
    v_s[c] = v
    kt_s[c] = k.T
    vt_s[c, :HEAD_DIM] = v.T
    vt_s[c, HEAD_DIM:] = jnp.ones((WIDE - HEAD_DIM, GROUP), BF)


def blocks(x):
    return x.reshape(ULY, ROWS, HEAD_DIM)


def flat(x):
    return x.reshape(GROUP, HEAD_DIM)


def main_kernel(pos_ref, qg_ref, prev_ref, own_ref, od_ref, back_k_ref, back_v_ref, mine_ref,
                k_s, v_s, kt_s, vt_s, dk_s, dv_s, s_s, p_s):
    gi = pl.program_id(0)
    z = pos_ref[0]

    @pl.when(gi == 0)
    def _():
        for c in range(QUAD):
            rows = slice(ULY * c, ULY * c + ULY)
            load_chunk(prev_ref.at[rows], c, k_s, v_s, kt_s, vt_s)
            load_chunk(own_ref.at[rows], QUAD + c, k_s, v_s, kt_s, vt_s)
        dk_s[:QUAD] = jnp.zeros((QUAD, GROUP, HEAD_DIM), F32)
        dv_s[:QUAD] = jnp.zeros((QUAD, GROUP, HEAD_DIM), F32)

    attend(lambda c: (z > 0) | (gi + c >= QUAD), gi, flat(qg_ref[:, 0]), flat(qg_ref[:, 1]), od_ref,
           k_s, v_s, kt_s, vt_s, dk_s, dv_s, s_s, p_s)
    back_k_ref[...] = blocks((dk_s[gi] * FACTOR).astype(BF))
    back_v_ref[...] = blocks(dv_s[gi].astype(BF))

    @pl.when(gi == QUAD - 1)
    def _():
        for c in range(QUAD):
            rows = slice(ULY * c, ULY * c + ULY)
            mine_ref[rows, 0] = blocks((dk_s[QUAD + c] * FACTOR).astype(BF))
            mine_ref[rows, 1] = blocks(dv_s[QUAD + c].astype(BF))


def fifth_kernel(flag_ref, all_ref, prev_ref, side_ref, core_ref, od_ref, mine_ref, b4_ref, b3_ref, b2_ref, b1_ref,
                 k_s, v_s, kt_s, vt_s, dk_s, dv_s, s_s, p_s):
    for c, ref in enumerate((prev_ref, side_ref, core_ref.at[0], core_ref.at[1], all_ref.at[:, 2:4])):
        load_chunk(ref, c, k_s, v_s, kt_s, vt_s)
    dk_s[:QUAD] = jnp.zeros((QUAD, GROUP, HEAD_DIM), F32)
    dv_s[:QUAD] = jnp.zeros((QUAD, GROUP, HEAD_DIM), F32)
    attend(lambda c: flag_ref[c] > 0, 0, flat(all_ref[:, 0]), flat(all_ref[:, 1]), od_ref,
           k_s, v_s, kt_s, vt_s, dk_s, dv_s, s_s, p_s)
    mine_ref[:, 0] = blocks(dk_s[WINDOW - 1] * FACTOR)
    mine_ref[:, 1] = blocks(dv_s[WINDOW - 1])
    far = jnp.where(flag_ref[4] == 0, 2, 3)
    for c, ref in ((0, b4_ref), (far, b3_ref), (1, b2_ref), (5 - far, b1_ref)):
        ref[:, 0] = blocks((dk_s[c] * FACTOR).astype(BF))
        ref[:, 1] = blocks(dv_s[c].astype(BF))


def scratch(chunks):
    return [
        pltpu.VMEM((chunks, GROUP, HEAD_DIM), BF),
        pltpu.VMEM((chunks, GROUP, HEAD_DIM), BF),
        pltpu.VMEM((chunks, HEAD_DIM, GROUP), BF),
        pltpu.VMEM((chunks, WIDE, GROUP), BF),
        pltpu.VMEM((chunks, GROUP, HEAD_DIM), F32),
        pltpu.VMEM((chunks, GROUP, HEAD_DIM), F32),
        pltpu.VMEM((WINDOW, GROUP, GROUP), F32),
        pltpu.VMEM((WINDOW, GROUP, GROUP), BF),
    ]


def cost(pairs):
    return pl.CostEstimate(flops=12 * pairs * GROUP * GROUP * HEAD_DIM,
                           bytes_accessed=pairs * 1000000, transcendentals=pairs * GROUP * GROUP)


def params(grid=False):
    return pltpu.CompilerParams(
        vmem_limit_bytes=56 * 2**20, dimension_semantics=("arbitrary",) if grid else None)


def bf(*dims):
    return jax.ShapeDtypeStruct((*dims, ROWS, HEAD_DIM), BF)


SMEM = pl.BlockSpec(memory_space=pltpu.SMEM)
VMEM = pl.BlockSpec(memory_space=pltpu.VMEM)
HBM = pl.BlockSpec(memory_space=pltpu.HBM)


def main_heads(pos, qg, prev, own):
    n = QUAD * ULY
    group = pl.BlockSpec((ULY, 2, ROWS, HEAD_DIM), lambda i: (i, 0, 0, 0))
    one = pl.BlockSpec((ULY, ROWS, HEAD_DIM), lambda i: (i, 0, 0))
    whole = pl.BlockSpec((n, 2, ROWS, HEAD_DIM), lambda i: (0, 0, 0, 0))
    return pl.pallas_call(
        main_kernel,
        out_shape=(bf(n, 2), bf(n), bf(n), bf(n, 2)),
        grid=(QUAD,),
        in_specs=[SMEM, group, whole, whole],
        out_specs=(group, one, one, whole),
        scratch_shapes=scratch(2 * QUAD),
        compiler_params=params(True),
        cost_estimate=cost(20),
        name="main_heads",
    )(pos, qg, prev, own)


def fifth_head(flags, mine, prev, side, core):
    return pl.pallas_call(
        fifth_kernel,
        out_shape=(bf(ULY, 2), jax.ShapeDtypeStruct((ULY, 2, ROWS, HEAD_DIM), F32)) + (bf(ULY, 2),) * 4,
        in_specs=[SMEM] + [VMEM] * 4,
        out_specs=(VMEM,) * 6,
        scratch_shapes=scratch(WINDOW),
        compiler_params=params(),
        cost_estimate=cost(5),
        name="fifth_head",
    )(flags, mine, prev, side, core)


def exchange(x, axes):
    return lax.all_to_all(x, axes, 0, 0, tiled=True)


def shifted(x, axes, size, distance):
    return lax.ppermute(x, axes, [(i - distance, i) for i in range(size) if 0 <= i - distance < size])


def pack_kernel(q_ref, g_ref, k_ref, v_ref, qg_ref, kv_ref):
    for i, ref in enumerate((q_ref, g_ref, k_ref, v_ref)):
        main_ref = qg_ref if i < 2 else kv_ref
        for u in range(ULY):
            for j in range(QUAD):
                col = (u * WINDOW + j) * HEAD_DIM
                main_ref[j * ULY + u, i % 2] = ref[:, col:col + HEAD_DIM]


def pack_fifth_kernel(q_ref, g_ref, k_ref, v_ref, fifth_ref, sem):
    copies = []
    for i, ref in enumerate((q_ref, g_ref, k_ref, v_ref)):
        for u in range(ULY):
            col = (u * WINDOW + QUAD) * HEAD_DIM
            copies.append(pltpu.make_async_copy(ref.at[:, pl.ds(col, HEAD_DIM)], fifth_ref.at[u, i], sem.at[i, u]))
    for copy in copies:
        copy.start()
    for copy in copies:
        copy.wait()


def unpack_kernel(first, main_ref, fifth_ref, *out_refs):
    for i, out_ref in enumerate(out_refs):
        for u in range(ULY):
            for j in range(WINDOW):
                col = (u * WINDOW + j) * HEAD_DIM
                out_ref[:, col:col + HEAD_DIM] = main_ref[j * ULY + u, i] if j < QUAD else fifth_ref[u, first + i]


def combine_kernel(mine_ref, k_ref, v_ref, out_ref):
    out_ref[:, 0] = (mine_ref[:, 0].astype(F32) + k_ref[...].astype(F32)).astype(BF)
    out_ref[:, 1] = (mine_ref[:, 1].astype(F32) + v_ref[...].astype(F32)).astype(BF)


def finish_kernel(od_ref, mine_ref, b4_ref, b3_ref, b2_ref, b1_ref, out_ref):
    out_ref[:, 0:2] = od_ref[...]
    total = mine_ref[...]
    for ref in (b4_ref, b3_ref, b2_ref, b1_ref):
        total = total + ref[...].astype(F32)
    out_ref[:, 2:4] = total.astype(BF)


def moved(kernel, name, out_shape, *arrays, limit=24):
    return pl.pallas_call(
        kernel,
        out_shape=tuple(out_shape),
        in_specs=[VMEM] * len(arrays),
        out_specs=(VMEM,) * len(out_shape),
        compiler_params=pltpu.CompilerParams(vmem_limit_bytes=limit * 2**20),
        cost_estimate=pl.CostEstimate(flops=0, bytes_accessed=2**22, transcendentals=0),
        name=name,
    )(*arrays)


def packed(*arrays):
    n = QUAD * ULY
    return moved(pack_kernel, "pack", [bf(n, 2)] * 2, *arrays, limit=56)


def packed_fifth(*arrays):
    return pl.pallas_call(
        pack_fifth_kernel,
        out_shape=bf(ULY, 4),
        in_specs=[HBM] * 4,
        out_specs=VMEM,
        scratch_shapes=[pltpu.SemaphoreType.DMA((4, ULY))],
        compiler_params=params(),
        cost_estimate=pl.CostEstimate(flops=0, bytes_accessed=2**21, transcendentals=0),
        name="pack_fifth",
    )(*arrays)


def unpacked(main, fifth, first):
    out = jax.ShapeDtypeStruct((ROWS, ULY * WINDOW * HEAD_DIM), BF)
    return moved(functools.partial(unpack_kernel, first), "unpack", [out] * 2, main, fifth)


def combined(*arrays):
    return moved(combine_kernel, "combine", [bf(QUAD * ULY, 2)], *arrays, limit=56)[0]


def swapped(x, axis):
    return lax.ppermute(x, axis, [(0, 1), (1, 0)])


def per_device(queries, keys, values, grad_out):
    z, xl, co = lax.axis_index("z"), lax.axis_index("xl"), lax.axis_index("co")
    fifth = exchange(packed_fifth(queries, grad_out, keys, values), COLUMN)
    qg, kv = packed(queries, grad_out, keys, values)
    fifth, kv = lax.optimization_barrier((fifth, kv))
    own = exchange(kv, PLANE)
    own5 = fifth[:, 2:4]
    prev5 = shifted(own5, "z", 4, 1)
    side5 = swapped(jnp.where(xl == 0, own5, prev5), "xl")
    core5 = swapped(jnp.stack([jnp.where(co == 0, own5, prev5), side5]), "co")
    later = (z > 0).astype(jnp.int32)
    side_ok, core_ok = jnp.maximum(later, xl), jnp.maximum(later, co)
    flags = jnp.stack([later, side_ok, core_ok, side_ok, co])
    own, qg = lax.optimization_barrier((own, qg))
    prev = shifted(own, "z", 4, 1)
    qg = exchange(qg, PLANE)

    od5, mine5, *back5 = fifth_head(flags, fifth, prev5, side5, core5)
    own, od5, mine5, *back5 = lax.optimization_barrier((own, od5, mine5, *back5))
    back5 = [shifted(part, TIME, 16, -d) for d, part in zip((4, 3, 2, 1), back5)]

    od, back_k, back_v, mine = main_heads(z.reshape(1), qg, prev, own)
    od, back_k, back_v, *back5 = lax.optimization_barrier((od, back_k, back_v, *back5))
    got_k = shifted(back_k, "z", 4, -1)
    got_v = shifted(back_v, "z", 4, -1)
    fifth = moved(finish_kernel, "finish", [bf(ULY, 4)], od5, mine5, *back5)[0]
    od, fifth = lax.optimization_barrier((od, fifth))
    od = exchange(od, PLANE)
    od, got_k, fifth, mine = lax.optimization_barrier((od, got_k, fifth, mine))
    fifth = exchange(fifth, COLUMN)
    fifth, dkv = lax.optimization_barrier((fifth, combined(mine, got_k, got_v)))
    dkv = exchange(dkv, PLANE)
    return (*unpacked(od, fifth, 0), *unpacked(dkv, fifth, 2))


def solution(mesh):
    fine = Mesh(mesh.devices.reshape(4, 2, 2, 4, 2), ALL)
    spec = P(ALL, None)
    return jax.shard_map(per_device, mesh=fine, in_specs=(spec,) * 4, out_specs=(spec,) * 4, check_vma=False)
```

```python
import functools
import math

import jax
import jax.numpy as jnp
from jax import lax
from jax.experimental import pallas as pl
from jax.experimental.pallas import tpu as pltpu
from jax.sharding import Mesh
from jax.sharding import PartitionSpec as P

HEAD_DIM = 128
WINDOW = 5
ROWS = 96
ULY = 8
QUAD = 4
GROUP = ROWS * ULY
WIDE = HEAD_DIM + 16
FACTOR = HEAD_DIM ** -0.5
LOG2E = math.log2(math.e)
PLANE = ("xl", "co", "y", "xh")
COLUMN = ("y", "xh")
TIME = ("z", "xl", "co")
ALL = ("z", "xl", "co", "y", "xh")
BF = jnp.bfloat16
F32 = jnp.float32


def dot(a, b, ca=1, cb=0):
    return lax.dot_general(a, b, (((ca,), (cb,)), ((), ())), preferred_element_type=F32)


def attend(allowed, gi, q, g, od_ref, k_s, v_s, kt_s, vt_s, dk_s, dv_s, s_s, p_s):
    top = jnp.full((8, GROUP), -jnp.inf, F32)
    for c in range(WINDOW):
        s = dot(k_s[gi + c], q, 1, 1)
        s_s[c] = s
        best = jnp.max(s.reshape(GROUP // 8, 8, GROUP), axis=0)
        if c < WINDOW - 1:
            best = jnp.where(allowed(c), best, -jnp.inf)
        top = jnp.maximum(top, best)
    top = jnp.max(top, axis=0, keepdims=True)
    for c in range(WINDOW):
        base = top if c == WINDOW - 1 else jnp.where(allowed(c), top, 1e30)
        p_s[c] = jnp.exp2((s_s[c] - base) * (FACTOR * LOG2E)).astype(BF)
    out_t = dot(jnp.concatenate([vt_s[gi + c] for c in range(WINDOW)], axis=1), p_s[...].reshape(WINDOW * GROUP, GROUP))
    inv = 1.0 / out_t[HEAD_DIM:HEAD_DIM + 1]
    out_t = out_t[:HEAD_DIM] * inv
    g_t = g.astype(F32).T
    row_dot = jnp.sum(g_t * out_t, axis=0, keepdims=True) * inv
    g_tb = (g_t * inv).astype(BF)
    g_b = g_tb.T
    od_ref[:, 0] = blocks(out_t.T.astype(BF))
    dq_t = jnp.zeros((HEAD_DIM, GROUP), F32)
    dp = dot(v_s[gi], g_tb)
    for c in range(WINDOW):
        pb = p_s[c]
        ds = (pb.astype(F32) * (dp - row_dot)).astype(BF)
        if c < WINDOW - 1:
            dp = dot(v_s[gi + c + 1], g_tb)
            dv_s[gi + c] += dot(pb, g_b)
            dk_s[gi + c] += dot(ds, q)
        else:
            dv_s[gi + c] = dot(pb, g_b)
            dk_s[gi + c] = dot(ds, q)
        dq_t = dq_t + dot(kt_s[gi + c], ds)
    od_ref[:, 1] = blocks((dq_t * FACTOR).T.astype(BF))


def load_chunk(kv_ref, c, k_s, v_s, kt_s, vt_s):
    k, v = flat(kv_ref[:, 0]), flat(kv_ref[:, 1])
    k_s[c] = k
    v_s[c] = v
    kt_s[c] = k.T
    vt_s[c, :HEAD_DIM] = v.T
    vt_s[c, HEAD_DIM:] = jnp.ones((WIDE - HEAD_DIM, GROUP), BF)


def blocks(x):
    return x.reshape(ULY, ROWS, HEAD_DIM)


def flat(x):
    return x.reshape(GROUP, HEAD_DIM)


def main_kernel(pos_ref, qg_ref, prev_ref, own_ref, od_ref, back_k_ref, back_v_ref, mine_ref,
                k_s, v_s, kt_s, vt_s, dk_s, dv_s, s_s, p_s):
    gi = pl.program_id(0)
    z = pos_ref[0]

    @pl.when(gi == 0)
    def _():
        for c in range(QUAD):
            rows = slice(ULY * c, ULY * c + ULY)
            load_chunk(prev_ref.at[rows], c, k_s, v_s, kt_s, vt_s)
            load_chunk(own_ref.at[rows], QUAD + c, k_s, v_s, kt_s, vt_s)
        dk_s[:QUAD] = jnp.zeros((QUAD, GROUP, HEAD_DIM), F32)
        dv_s[:QUAD] = jnp.zeros((QUAD, GROUP, HEAD_DIM), F32)

    attend(lambda c: (z > 0) | (gi + c >= QUAD), gi, flat(qg_ref[:, 0]), flat(qg_ref[:, 1]), od_ref,
           k_s, v_s, kt_s, vt_s, dk_s, dv_s, s_s, p_s)
    back_k_ref[...] = blocks((dk_s[gi] * FACTOR).astype(BF))
    back_v_ref[...] = blocks(dv_s[gi].astype(BF))

    @pl.when(gi == QUAD - 1)
    def _():
        for c in range(QUAD):
            rows = slice(ULY * c, ULY * c + ULY)
            mine_ref[rows, 0] = blocks((dk_s[QUAD + c] * FACTOR).astype(BF))
            mine_ref[rows, 1] = blocks(dv_s[QUAD + c].astype(BF))


def fifth_kernel(flag_ref, all_ref, prev_ref, side_ref, core_ref, od_ref, mine_ref, b4_ref, b3_ref, b2_ref, b1_ref,
                 k_s, v_s, kt_s, vt_s, dk_s, dv_s, s_s, p_s):
    for c, ref in enumerate((prev_ref, side_ref, core_ref.at[0], core_ref.at[1], all_ref.at[:, 2:4])):
        load_chunk(ref, c, k_s, v_s, kt_s, vt_s)
    dk_s[:QUAD] = jnp.zeros((QUAD, GROUP, HEAD_DIM), F32)
    dv_s[:QUAD] = jnp.zeros((QUAD, GROUP, HEAD_DIM), F32)
    attend(lambda c: flag_ref[c] > 0, 0, flat(all_ref[:, 0]), flat(all_ref[:, 1]), od_ref,
           k_s, v_s, kt_s, vt_s, dk_s, dv_s, s_s, p_s)
    mine_ref[:, 0] = blocks(dk_s[WINDOW - 1] * FACTOR)
    mine_ref[:, 1] = blocks(dv_s[WINDOW - 1])
    far = jnp.where(flag_ref[4] == 0, 2, 3)
    for c, ref in ((0, b4_ref), (far, b3_ref), (1, b2_ref), (5 - far, b1_ref)):
        ref[:, 0] = blocks((dk_s[c] * FACTOR).astype(BF))
        ref[:, 1] = blocks(dv_s[c].astype(BF))


def scratch(chunks):
    return [
        pltpu.VMEM((chunks, GROUP, HEAD_DIM), BF),
        pltpu.VMEM((chunks, GROUP, HEAD_DIM), BF),
        pltpu.VMEM((chunks, HEAD_DIM, GROUP), BF),
        pltpu.VMEM((chunks, WIDE, GROUP), BF),
        pltpu.VMEM((chunks, GROUP, HEAD_DIM), F32),
        pltpu.VMEM((chunks, GROUP, HEAD_DIM), F32),
        pltpu.VMEM((WINDOW, GROUP, GROUP), F32),
        pltpu.VMEM((WINDOW, GROUP, GROUP), BF),
    ]


def cost(pairs):
    return pl.CostEstimate(flops=12 * pairs * GROUP * GROUP * HEAD_DIM,
                           bytes_accessed=pairs * 1000000, transcendentals=pairs * GROUP * GROUP)


def params(grid=False):
    return pltpu.CompilerParams(
        vmem_limit_bytes=56 * 2**20, dimension_semantics=("arbitrary",) if grid else None)


def bf(*dims):
    return jax.ShapeDtypeStruct((*dims, ROWS, HEAD_DIM), BF)


SMEM = pl.BlockSpec(memory_space=pltpu.SMEM)
VMEM = pl.BlockSpec(memory_space=pltpu.VMEM)
HBM = pl.BlockSpec(memory_space=pltpu.HBM)


def main_heads(pos, qg, prev, own):
    n = QUAD * ULY
    group = pl.BlockSpec((ULY, 2, ROWS, HEAD_DIM), lambda i: (i, 0, 0, 0))
    one = pl.BlockSpec((ULY, ROWS, HEAD_DIM), lambda i: (i, 0, 0))
    whole = pl.BlockSpec((n, 2, ROWS, HEAD_DIM), lambda i: (0, 0, 0, 0))
    return pl.pallas_call(
        main_kernel,
        out_shape=(bf(n, 2), bf(n), bf(n), bf(n, 2)),
        grid=(QUAD,),
        in_specs=[SMEM, group, whole, whole],
        out_specs=(group, one, one, whole),
        scratch_shapes=scratch(2 * QUAD),
        compiler_params=params(True),
        cost_estimate=cost(20),
        name="main_heads",
    )(pos, qg, prev, own)


def fifth_head(flags, mine, prev, side, core):
    return pl.pallas_call(
        fifth_kernel,
        out_shape=(bf(ULY, 2), jax.ShapeDtypeStruct((ULY, 2, ROWS, HEAD_DIM), F32)) + (bf(ULY, 2),) * 4,
        in_specs=[SMEM] + [VMEM] * 4,
        out_specs=(VMEM,) * 6,
        scratch_shapes=scratch(WINDOW),
        compiler_params=params(),
        cost_estimate=cost(5),
        name="fifth_head",
    )(flags, mine, prev, side, core)


def exchange(x, axes):
    return lax.all_to_all(x, axes, 0, 0, tiled=True)


def shifted(x, axes, size, distance):
    return lax.ppermute(x, axes, [(i - distance, i) for i in range(size) if 0 <= i - distance < size])


def pack_kernel(q_ref, g_ref, k_ref, v_ref, qg_ref, kv_ref):
    for i, ref in enumerate((q_ref, g_ref, k_ref, v_ref)):
        main_ref = qg_ref if i < 2 else kv_ref
        for u in range(ULY):
            for j in range(QUAD):
                col = (u * WINDOW + j) * HEAD_DIM
                main_ref[j * ULY + u, i % 2] = ref[:, col:col + HEAD_DIM]


def pack_fifth_kernel(q_ref, g_ref, k_ref, v_ref, fifth_ref, sem):
    copies = []
    for i, ref in enumerate((q_ref, g_ref, k_ref, v_ref)):
        for u in range(ULY):
            col = (u * WINDOW + QUAD) * HEAD_DIM
            copies.append(pltpu.make_async_copy(ref.at[:, pl.ds(col, HEAD_DIM)], fifth_ref.at[u, i], sem.at[i, u]))
    for copy in copies:
        copy.start()
    for copy in copies:
        copy.wait()


def unpack_kernel(first, main_ref, fifth_ref, *out_refs):
    for i, out_ref in enumerate(out_refs):
        for u in range(ULY):
            for j in range(WINDOW):
                col = (u * WINDOW + j) * HEAD_DIM
                out_ref[:, col:col + HEAD_DIM] = main_ref[j * ULY + u, i] if j < QUAD else fifth_ref[u, first + i]


def combine_kernel(mine_ref, k_ref, v_ref, out_ref):
    out_ref[:, 0] = (mine_ref[:, 0].astype(F32) + k_ref[...].astype(F32)).astype(BF)
    out_ref[:, 1] = (mine_ref[:, 1].astype(F32) + v_ref[...].astype(F32)).astype(BF)


def finish_kernel(od_ref, mine_ref, b4_ref, b3_ref, b2_ref, b1_ref, out_ref):
    out_ref[:, 0:2] = od_ref[...]
    total = mine_ref[...]
    for ref in (b4_ref, b3_ref, b2_ref, b1_ref):
        total = total + ref[...].astype(F32)
    out_ref[:, 2:4] = total.astype(BF)


def moved(kernel, name, out_shape, *arrays, limit=24):
    return pl.pallas_call(
        kernel,
        out_shape=tuple(out_shape),
        in_specs=[VMEM] * len(arrays),
        out_specs=(VMEM,) * len(out_shape),
        compiler_params=pltpu.CompilerParams(vmem_limit_bytes=limit * 2**20),
        cost_estimate=pl.CostEstimate(flops=0, bytes_accessed=2**22, transcendentals=0),
        name=name,
    )(*arrays)


def packed(*arrays):
    n = QUAD * ULY
    return moved(pack_kernel, "pack", [bf(n, 2)] * 2, *arrays, limit=56)


def packed_fifth(*arrays):
    return pl.pallas_call(
        pack_fifth_kernel,
        out_shape=bf(ULY, 4),
        in_specs=[HBM] * 4,
        out_specs=VMEM,
        scratch_shapes=[pltpu.SemaphoreType.DMA((4, ULY))],
        compiler_params=params(),
        cost_estimate=pl.CostEstimate(flops=0, bytes_accessed=2**21, transcendentals=0),
        name="pack_fifth",
    )(*arrays)


def unpacked(main, fifth, first):
    out = jax.ShapeDtypeStruct((ROWS, ULY * WINDOW * HEAD_DIM), BF)
    return moved(functools.partial(unpack_kernel, first), "unpack", [out] * 2, main, fifth)


def combined(*arrays):
    return moved(combine_kernel, "combine", [bf(QUAD * ULY, 2)], *arrays, limit=56)[0]


def swapped(x, axis):
    return lax.ppermute(x, axis, [(0, 1), (1, 0)])


def per_device(queries, keys, values, grad_out):
    z, xl, co = lax.axis_index("z"), lax.axis_index("xl"), lax.axis_index("co")
    fifth = exchange(packed_fifth(queries, grad_out, keys, values), COLUMN)
    qg, kv = packed(queries, grad_out, keys, values)
    fifth, kv = lax.optimization_barrier((fifth, kv))
    own = exchange(kv, PLANE)
    own5 = fifth[:, 2:4]
    prev5 = shifted(own5, "z", 4, 1)
    side5 = swapped(jnp.where(xl == 0, own5, prev5), "xl")
    core5 = swapped(jnp.stack([jnp.where(co == 0, own5, prev5), side5]), "co")
    later = (z > 0).astype(jnp.int32)
    side_ok, core_ok = jnp.maximum(later, xl), jnp.maximum(later, co)
    flags = jnp.stack([later, side_ok, core_ok, side_ok, co])
    own, qg = lax.optimization_barrier((own, qg))
    prev = shifted(own, "z", 4, 1)
    qg = exchange(qg, PLANE)

    od5, mine5, *back5 = fifth_head(flags, fifth, prev5, side5, core5)
    own, od5, mine5, *back5 = lax.optimization_barrier((own, od5, mine5, *back5))
    back5 = [shifted(part, TIME, 16, -d) for d, part in zip((4, 3, 2, 1), back5)]

    od, back_k, back_v, mine = main_heads(z.reshape(1), qg, prev, own)
    od, back_k, back_v, *back5 = lax.optimization_barrier((od, back_k, back_v, *back5))
    got_k = shifted(back_k, "z", 4, -1)
    got_v = shifted(back_v, "z", 4, -1)
    fifth = moved(finish_kernel, "finish", [bf(ULY, 4)], od5, mine5, *back5)[0]
    od, fifth = lax.optimization_barrier((od, fifth))
    od = exchange(od, PLANE)
    od, got_k, fifth, mine = lax.optimization_barrier((od, got_k, fifth, mine))
    fifth = exchange(fifth, COLUMN)
    fifth, dkv = lax.optimization_barrier((fifth, combined(mine, got_k, got_v)))
    dkv = exchange(dkv, PLANE)
    return (*unpacked(od, fifth, 0), *unpacked(dkv, fifth, 2))


def solution(mesh):
    fine = Mesh(mesh.devices.reshape(4, 2, 2, 4, 2), ALL)
    spec = P(ALL, None)
    return jax.shard_map(per_device, mesh=fine, in_specs=(spec,) * 4, out_specs=(spec,) * 4, check_vma=False)
```

```python
import functools
import math

import jax
import jax.numpy as jnp
from jax import lax
from jax.experimental import pallas as pl
from jax.experimental.pallas import tpu as pltpu
from jax.sharding import Mesh
from jax.sharding import PartitionSpec as P

HEAD_DIM = 128
WINDOW = 5
ROWS = 96
ULY = 8
QUAD = 4
GROUP = ROWS * ULY
WIDE = HEAD_DIM + 16
FACTOR = HEAD_DIM ** -0.5
LOG2E = math.log2(math.e)
PLANE = ("xl", "co", "y", "xh")
COLUMN = ("y", "xh")
TIME = ("z", "xl", "co")
ALL = ("z", "xl", "co", "y", "xh")
BF = jnp.bfloat16
F32 = jnp.float32


def dot(a, b, ca=1, cb=0):
    return lax.dot_general(a, b, (((ca,), (cb,)), ((), ())), preferred_element_type=F32)


def attend(allowed, gi, q, g, od_ref, k_s, v_s, kt_s, vt_s, dk_s, dv_s, s_s, p_s, d_s):
    top = jnp.full((8, GROUP), -jnp.inf, F32)
    tops = [top[:, :GROUP // 3]] * 3
    for c in range(WINDOW):
        for i in range(3):
            part = slice(i * GROUP // 3, (i + 1) * GROUP // 3)
            s = dot(k_s[gi + c], q[part], 1, 1)
            s_s[c, :, part] = s
            best = jnp.max(s.reshape(GROUP // 8, 8, GROUP // 3), axis=0)
            if c < WINDOW - 1:
                best = jnp.where(allowed(c), best, -jnp.inf)
            tops[i] = jnp.maximum(tops[i], best)
    top = jnp.concatenate(tops, axis=1)
    top = jnp.max(top, axis=0, keepdims=True)
    for c in range(WINDOW):
        base = top if c == WINDOW - 1 else jnp.where(allowed(c), top, 1e30)
        p_s[c] = jnp.exp2((s_s[c] - base) * (FACTOR * LOG2E)).astype(BF)
    out_t = dot(jnp.concatenate([vt_s[gi + c] for c in range(WINDOW)], axis=1), p_s[...].reshape(WINDOW * GROUP, GROUP))
    inv = 1.0 / out_t[HEAD_DIM:HEAD_DIM + 1]
    out_t = out_t[:HEAD_DIM] * inv
    g_t = g.astype(F32).T
    row_dot = jnp.sum(g_t * out_t, axis=0, keepdims=True) * inv
    g_tb = (g_t * inv).astype(BF)
    g_b = g_tb.T
    od_ref[:, 0] = blocks(out_t.T.astype(BF))
    dq_t = jnp.zeros((HEAD_DIM, GROUP), F32)
    dp = dot(v_s[gi], g_tb)
    for c in range(WINDOW):
        pb = p_s[c]
        d_s[c] = (pb.astype(F32) * (dp - row_dot)).astype(BF)
        if c < WINDOW - 1:
            dp = dot(v_s[gi + c + 1], g_tb)
            dv_s[gi + c] += dot(pb, g_b)
            dk_s[gi + c] += dot(d_s[c], q)
        else:
            dv_s[gi + c] = dot(pb, g_b)
            dk_s[gi + c] = dot(d_s[c], q)
    dq_t = dot(jnp.concatenate([kt_s[gi + c] for c in range(WINDOW)], axis=1), d_s[...].reshape(WINDOW * GROUP, GROUP))
    od_ref[:, 1] = blocks((dq_t * FACTOR).T.astype(BF))


def load_chunk(kv_ref, c, k_s, v_s, kt_s, vt_s):
    k, v = flat(kv_ref[:, 0]), flat(kv_ref[:, 1])
    k_s[c] = k
    v_s[c] = v
    kt_s[c] = k.T
    vt_s[c, :HEAD_DIM] = v.T
    vt_s[c, HEAD_DIM:] = jnp.ones((WIDE - HEAD_DIM, GROUP), BF)


def blocks(x):
    return x.reshape(ULY, ROWS, HEAD_DIM)


def flat(x):
    return x.reshape(GROUP, HEAD_DIM)


def main_kernel(pos_ref, qg_ref, prev_ref, own_ref, od_ref, back_k_ref, back_v_ref, mine_ref,
                k_s, v_s, kt_s, vt_s, dk_s, dv_s, s_s, p_s, d_s):
    gi = pl.program_id(0)
    z = pos_ref[0]

    @pl.when(gi == 0)
    def _():
        for c in range(QUAD):
            rows = slice(ULY * c, ULY * c + ULY)
            load_chunk(prev_ref.at[rows], c, k_s, v_s, kt_s, vt_s)
            load_chunk(own_ref.at[rows], QUAD + c, k_s, v_s, kt_s, vt_s)
        dk_s[:QUAD] = jnp.zeros((QUAD, GROUP, HEAD_DIM), F32)
        dv_s[:QUAD] = jnp.zeros((QUAD, GROUP, HEAD_DIM), F32)

    attend(lambda c: (z > 0) | (gi + c >= QUAD), gi, flat(qg_ref[:, 0]), flat(qg_ref[:, 1]), od_ref,
           k_s, v_s, kt_s, vt_s, dk_s, dv_s, s_s, p_s, d_s)
    back_k_ref[...] = blocks((dk_s[gi] * FACTOR).astype(BF))
    back_v_ref[...] = blocks(dv_s[gi].astype(BF))

    @pl.when(gi == QUAD - 1)
    def _():
        for c in range(QUAD):
            rows = slice(ULY * c, ULY * c + ULY)
            mine_ref[rows, 0] = blocks((dk_s[QUAD + c] * FACTOR).astype(BF))
            mine_ref[rows, 1] = blocks(dv_s[QUAD + c].astype(BF))


def fifth_kernel(flag_ref, all_ref, prev_ref, side_ref, core_ref, od_ref, mine_ref, b4_ref, b3_ref, b2_ref, b1_ref,
                 k_s, v_s, kt_s, vt_s, dk_s, dv_s, s_s, p_s, d_s):
    for c, ref in enumerate((prev_ref, side_ref, core_ref.at[0], core_ref.at[1], all_ref.at[:, 2:4])):
        load_chunk(ref, c, k_s, v_s, kt_s, vt_s)
    dk_s[:QUAD] = jnp.zeros((QUAD, GROUP, HEAD_DIM), F32)
    dv_s[:QUAD] = jnp.zeros((QUAD, GROUP, HEAD_DIM), F32)
    attend(lambda c: flag_ref[c] > 0, 0, flat(all_ref[:, 0]), flat(all_ref[:, 1]), od_ref,
           k_s, v_s, kt_s, vt_s, dk_s, dv_s, s_s, p_s, d_s)
    mine_ref[:, 0] = blocks(dk_s[WINDOW - 1] * FACTOR)
    mine_ref[:, 1] = blocks(dv_s[WINDOW - 1])
    far = jnp.where(flag_ref[4] == 0, 2, 3)
    for c, ref in ((0, b4_ref), (far, b3_ref), (1, b2_ref), (5 - far, b1_ref)):
        ref[:, 0] = blocks((dk_s[c] * FACTOR).astype(BF))
        ref[:, 1] = blocks(dv_s[c].astype(BF))


def scratch(chunks):
    return [
        pltpu.VMEM((chunks, GROUP, HEAD_DIM), BF),
        pltpu.VMEM((chunks, GROUP, HEAD_DIM), BF),
        pltpu.VMEM((chunks, HEAD_DIM, GROUP), BF),
        pltpu.VMEM((chunks, WIDE, GROUP), BF),
        pltpu.VMEM((chunks, GROUP, HEAD_DIM), F32),
        pltpu.VMEM((chunks, GROUP, HEAD_DIM), F32),
        pltpu.VMEM((WINDOW, GROUP, GROUP), F32),
        pltpu.VMEM((WINDOW, GROUP, GROUP), BF),
        pltpu.VMEM((WINDOW, GROUP, GROUP), BF),
    ]


def cost(pairs):
    return pl.CostEstimate(flops=12 * pairs * GROUP * GROUP * HEAD_DIM,
                           bytes_accessed=pairs * 1000000, transcendentals=pairs * GROUP * GROUP)


def params(grid=False):
    return pltpu.CompilerParams(
        vmem_limit_bytes=56 * 2**20, dimension_semantics=("arbitrary",) if grid else None)


def bf(*dims):
    return jax.ShapeDtypeStruct((*dims, ROWS, HEAD_DIM), BF)


SMEM = pl.BlockSpec(memory_space=pltpu.SMEM)
VMEM = pl.BlockSpec(memory_space=pltpu.VMEM)
HBM = pl.BlockSpec(memory_space=pltpu.HBM)


def main_heads(pos, qg, prev, own):
    n = QUAD * ULY
    group = pl.BlockSpec((ULY, 2, ROWS, HEAD_DIM), lambda i: (i, 0, 0, 0))
    one = pl.BlockSpec((ULY, ROWS, HEAD_DIM), lambda i: (i, 0, 0))
    whole = pl.BlockSpec((n, 2, ROWS, HEAD_DIM), lambda i: (0, 0, 0, 0))
    return pl.pallas_call(
        main_kernel,
        out_shape=(bf(n, 2), bf(n), bf(n), bf(n, 2)),
        grid=(QUAD,),
        in_specs=[SMEM, group, whole, whole],
        out_specs=(group, one, one, whole),
        scratch_shapes=scratch(2 * QUAD),
        compiler_params=params(True),
        cost_estimate=cost(20),
        name="main_heads",
    )(pos, qg, prev, own)


def fifth_head(flags, mine, prev, side, core):
    return pl.pallas_call(
        fifth_kernel,
        out_shape=(bf(ULY, 2), jax.ShapeDtypeStruct((ULY, 2, ROWS, HEAD_DIM), F32)) + (bf(ULY, 2),) * 4,
        in_specs=[SMEM] + [VMEM] * 4,
        out_specs=(VMEM,) * 6,
        scratch_shapes=scratch(WINDOW),
        compiler_params=params(),
        cost_estimate=cost(5),
        name="fifth_head",
    )(flags, mine, prev, side, core)


def exchange(x, axes):
    return lax.all_to_all(x, axes, 0, 0, tiled=True)


def shifted(x, axes, size, distance):
    return lax.ppermute(x, axes, [(i - distance, i) for i in range(size) if 0 <= i - distance < size])


def pack_kernel(q_ref, g_ref, k_ref, v_ref, qg_ref, kv_ref):
    for i, ref in enumerate((q_ref, g_ref, k_ref, v_ref)):
        main_ref = qg_ref if i < 2 else kv_ref
        for u in range(ULY):
            for j in range(QUAD):
                col = (u * WINDOW + j) * HEAD_DIM
                main_ref[j * ULY + u, i % 2] = ref[:, col:col + HEAD_DIM]


def pack_fifth_kernel(q_ref, g_ref, k_ref, v_ref, fifth_ref, sem):
    copies = []
    for i, ref in enumerate((q_ref, g_ref, k_ref, v_ref)):
        for u in range(ULY):
            col = (u * WINDOW + QUAD) * HEAD_DIM
            copies.append(pltpu.make_async_copy(ref.at[:, pl.ds(col, HEAD_DIM)], fifth_ref.at[u, i], sem.at[i, u]))
    for copy in copies:
        copy.start()
    for copy in copies:
        copy.wait()


def unpack_kernel(first, main_ref, fifth_ref, *out_refs):
    for i, out_ref in enumerate(out_refs):
        for u in range(ULY):
            for j in range(WINDOW):
                col = (u * WINDOW + j) * HEAD_DIM
                out_ref[:, col:col + HEAD_DIM] = main_ref[j * ULY + u, i] if j < QUAD else fifth_ref[u, first + i]


def combine_kernel(mine_ref, k_ref, v_ref, out_ref):
    out_ref[:, 0] = (mine_ref[:, 0].astype(F32) + k_ref[...].astype(F32)).astype(BF)
    out_ref[:, 1] = (mine_ref[:, 1].astype(F32) + v_ref[...].astype(F32)).astype(BF)


def finish_kernel(od_ref, mine_ref, b4_ref, b3_ref, b2_ref, b1_ref, out_ref):
    out_ref[:, 0:2] = od_ref[...]
    total = mine_ref[...]
    for ref in (b4_ref, b3_ref, b2_ref, b1_ref):
        total = total + ref[...].astype(F32)
    out_ref[:, 2:4] = total.astype(BF)


def moved(kernel, name, out_shape, *arrays, limit=24):
    return pl.pallas_call(
        kernel,
        out_shape=tuple(out_shape),
        in_specs=[VMEM] * len(arrays),
        out_specs=(VMEM,) * len(out_shape),
        compiler_params=pltpu.CompilerParams(vmem_limit_bytes=limit * 2**20),
        cost_estimate=pl.CostEstimate(flops=0, bytes_accessed=2**22, transcendentals=0),
        name=name,
    )(*arrays)


def packed(*arrays):
    n = QUAD * ULY
    return moved(pack_kernel, "pack", [bf(n, 2)] * 2, *arrays, limit=56)


def packed_fifth(*arrays):
    return pl.pallas_call(
        pack_fifth_kernel,
        out_shape=bf(ULY, 4),
        in_specs=[HBM] * 4,
        out_specs=VMEM,
        scratch_shapes=[pltpu.SemaphoreType.DMA((4, ULY))],
        compiler_params=params(),
        cost_estimate=pl.CostEstimate(flops=0, bytes_accessed=2**21, transcendentals=0),
        name="pack_fifth",
    )(*arrays)


def unpacked(main, fifth, first):
    out = jax.ShapeDtypeStruct((ROWS, ULY * WINDOW * HEAD_DIM), BF)
    return moved(functools.partial(unpack_kernel, first), "unpack", [out] * 2, main, fifth)


def combined(*arrays):
    return moved(combine_kernel, "combine", [bf(QUAD * ULY, 2)], *arrays, limit=56)[0]


def swapped(x, axis):
    return lax.ppermute(x, axis, [(0, 1), (1, 0)])


def per_device(queries, keys, values, grad_out):
    z, xl, co = lax.axis_index("z"), lax.axis_index("xl"), lax.axis_index("co")
    fifth = exchange(packed_fifth(queries, grad_out, keys, values), COLUMN)
    qg, kv = packed(queries, grad_out, keys, values)
    fifth, kv = lax.optimization_barrier((fifth, kv))
    own = exchange(kv, PLANE)
    own5 = fifth[:, 2:4]
    prev5 = shifted(own5, "z", 4, 1)
    side5 = swapped(jnp.where(xl == 0, own5, prev5), "xl")
    core5 = swapped(jnp.stack([jnp.where(co == 0, own5, prev5), side5]), "co")
    later = (z > 0).astype(jnp.int32)
    side_ok, core_ok = jnp.maximum(later, xl), jnp.maximum(later, co)
    flags = jnp.stack([later, side_ok, core_ok, side_ok, co])
    own, qg = lax.optimization_barrier((own, qg))
    prev = shifted(own, "z", 4, 1)
    qg = exchange(qg, PLANE)

    od5, mine5, *back5 = fifth_head(flags, fifth, prev5, side5, core5)
    own, od5, mine5, *back5 = lax.optimization_barrier((own, od5, mine5, *back5))
    back5 = [shifted(part, TIME, 16, -d) for d, part in zip((4, 3, 2, 1), back5)]

    od, back_k, back_v, mine = main_heads(z.reshape(1), qg, prev, own)
    od, back_k, back_v, *back5 = lax.optimization_barrier((od, back_k, back_v, *back5))
    got_k = shifted(back_k, "z", 4, -1)
    got_v = shifted(back_v, "z", 4, -1)
    fifth = moved(finish_kernel, "finish", [bf(ULY, 4)], od5, mine5, *back5)[0]
    od, fifth = lax.optimization_barrier((od, fifth))
    od = exchange(od, PLANE)
    od, got_k, fifth, mine = lax.optimization_barrier((od, got_k, fifth, mine))
    fifth = exchange(fifth, COLUMN)
    fifth, dkv = lax.optimization_barrier((fifth, combined(mine, got_k, got_v)))
    dkv = exchange(dkv, PLANE)
    return (*unpacked(od, fifth, 0), *unpacked(dkv, fifth, 2))


def solution(mesh):
    fine = Mesh(mesh.devices.reshape(4, 2, 2, 4, 2), ALL)
    spec = P(ALL, None)
    return jax.shard_map(per_device, mesh=fine, in_specs=(spec,) * 4, out_specs=(spec,) * 4, check_vma=False)
```
